1024 devices in a mesh: dp: 32 (over z), expert: 32 (over y, x, core).
Axes of the slice: x: 4, y: 4, z: 32, core: 2. Of those that a mesh axis runs over, the one named last changes fastest.
Arguments:
- tokens: bfloat16 [32768, 4096], P('dp', 'expert'), may hold values from -6 to 6
- cotangent: bfloat16 [32768, 4096], P('dp', 'expert'), may hold values from -6 to 6
- expert_ids: int32 [32768, 8], P('dp'), may hold values from 0 to 127, all different within a row; in each aligned block of 1024 rows (0 to 1023, 1024 to 2047, ...) at most 128 rows name the same one
- gate_values: float32 [32768, 8], P('dp'), may hold values from 0.05 to 0.5
- gate_proj: bfloat16 [6144, 4096], P('expert'), may hold values from -0.09375 to 0.09375
- up_proj: bfloat16 [6144, 4096], P('expert'), may hold values from -0.09375 to 0.09375
- down_proj: bfloat16 [6144, 4096], P('expert'), may hold values from -0.15625 to 0.15625
- probe: bfloat16 [6144, 4096], P('expert'), may hold values from -0.09375 to 0.09375
Outputs:
- hessian_probe: bfloat16 [6144, 4096], P('expert', 'dp')
The draws below stay inside these ranges and needn't reach their ends.
Inputs may be any that keep to these rules, and one draw needn't show every extreme that they name: `expert_ids`: each row names 8 different experts. In each aligned block of 1024 rows (the rows of one index of dp) no expert is named by more than 128 rows, a bound that some block reaches.
All inputs are finite; a program needn't handle non-finite values.
Results may differ from the reference program's by a relative error of at most 0.0058.
Values may be sent and summed in bfloat16 or wider, within the bound.
No kernel may reach another device: no remote copies, remote signals or barrier semaphores. Data moves between devices by JAX's collectives and lax.ppermute only.
A program may use at most 32 MiB of HBM per device.

```python
import math
import jax
import jax.numpy as jnp
import numpy as np
from jax import lax

D = 4096
FF = 1536
EXPERTS = 128
TOPK = 8
TOK_ROW = 1024
EXP_WIN = 4
HIDDEN_SIZE = 6144
CAP = 128
TOKENS = 32768
N_DP = 32


def levels(stream_key, dims, shards, smallest, high):
    gain = 1.0
    for position, shards_of in shards:
        steps = jax.random.uniform(jax.random.fold_in(jax.random.fold_in(stream_key, 6), position), (shards_of,), jnp.float32, smallest / len(shards), high / len(shards))
        gain = gain * jnp.repeat(jnp.exp(steps), dims[position] // shards_of).reshape((-1,) + (1,) * (len(dims) - 1 - position))
    return gain


def assign_block(stream_key, own, number, rows, number_of, top, bound, lean):
    sequence = jax.random.permutation(stream_key, number_of)
    crowded, usual = shares(number_of, rows * top, bound, lean, True), shares(number_of, rows * top, bound, lean, False)
    places = jnp.arange(number_of)

    def named(tallies, offset_by):
        used = int((tallies > 0).sum())
        fixed = max(1, used // 4)
        shifted = fixed + (places - fixed + offset_by * (used - fixed)) % max(1, number_of - fixed)
        return jnp.zeros((number_of,), jnp.int32).at[sequence[jnp.where(places < fixed, places, shifted)]].set(jnp.asarray(tallies, jnp.int32))

    tallies = jnp.where(number % 4 == 0, named(crowded, number // 4), named(usual, number - number // 4 - 1))
    mixed = jax.random.permutation(jax.random.fold_in(own, 3), number_of)
    giver, receiver = mixed[0:number_of // 2 * 2:2], mixed[1:number_of // 2 * 2:2]
    margin = jnp.minimum(tallies[giver] - 1, bound - tallies[receiver]) // 2
    margin = jnp.where((giver == sequence[0]) | (receiver == sequence[0]) | (tallies[receiver] == 0), 0, jnp.maximum(margin, 0))
    shifted = jax.random.randint(jax.random.fold_in(own, 4), (number_of // 2,), 0, 1 << 20) % (margin + 1)
    tallies = tallies.at[giver].add(-shifted).at[receiver].add(shifted)
    items = jnp.searchsorted(jnp.cumsum(tallies), jnp.arange(rows * top), side="right").astype(jnp.int32)
    listing = items.reshape(top, rows).T
    listing = listing[jax.random.permutation(jax.random.fold_in(own, 1), rows)]
    offset_by = jax.random.randint(jax.random.fold_in(own, 2), (rows, 1), 0, top)
    return jnp.take_along_axis(listing, (jnp.arange(top)[None, :] + offset_by) % top, axis=1)


def shares(number_of, total, reach, skew, full):
    portions = [(1 << 20) // math.isqrt(grade ** skew) + 1 for grade in range(1, number_of + 1)]
    largest = reach if full else min(reach, max(-(-total // number_of), total * portions[0] // sum(portions)))
    least = 1 if total - largest >= number_of - 1 else 0
    holding, surplus = [largest] + [least] * (number_of - 1), total - largest - least * (number_of - 1)
    while surplus > 0:
        free = [i for i in range(1, number_of) if holding[i] < largest] or [i for i in range(1, number_of) if holding[i] < reach]
        pool, budget = sum([portions[i] for i in free]), surplus
        for i in free:
            addition = min(reach - holding[i], max(1, budget * portions[i] // pool), surplus)
            holding[i] = holding[i] + addition
            surplus = surplus - addition
    return np.array(holding)


def bell_draw(rng, shape, deviation, limit, split=(), kind=jnp.bfloat16):
    gain = levels(rng, shape, split, -0.22, 0.18) if split else 1.0
    values = jax.random.normal(rng, shape, jnp.float32) * deviation * gain
    return jnp.minimum(jnp.maximum(values, -limit), limit).astype(kind)


def setup_inputs(seed: int = 0) -> dict:
    key_list = jax.random.split(jax.random.key(seed), 9)
    tokens = bell_draw(key_list[0], (TOKENS, D), 1.0, 6.0, ((0, 32), (1, 32)))
    cotangent = bell_draw(key_list[1], (TOKENS, D), 1.0, 6.0, ((0, 32), (1, 32)))
    expert_ids_keys = jax.random.split(jax.random.fold_in(key_list[2], 1), TOKENS // TOK_ROW)
    expert_ids_turns = jax.random.permutation(jax.random.fold_in(key_list[2], 3), TOKENS // TOK_ROW)
    expert_ids = jax.vmap(lambda own, number: assign_block(jax.random.fold_in(key_list[2], 2), own, number, TOK_ROW, EXPERTS, TOPK, CAP, 2))(expert_ids_keys, expert_ids_turns).reshape((TOKENS, TOPK))
    gate_values = jnp.clip(jnp.exp(math.log(0.5) - 2.3025851 * jax.random.uniform(key_list[3], (TOKENS, TOPK), jnp.float32) ** levels(key_list[3], (TOKENS, TOPK), ((0, 32),), -0.2, 0.2)), 0.05, 0.5)
    gate_proj = bell_draw(key_list[4], (HIDDEN_SIZE, D), D ** -0.5, 0.09375, ((0, 32),))
    up_proj = bell_draw(key_list[5], (HIDDEN_SIZE, D), D ** -0.5, 0.09375, ((0, 32),))
    down_proj = bell_draw(key_list[6], (HIDDEN_SIZE, D), FF ** -0.5, 0.15625, ((0, 32),))
    probe = bell_draw(key_list[7], (HIDDEN_SIZE, D), D ** -0.5, 0.09375, ((0, 32),))
    return {"tokens": tokens, "cotangent": cotangent, "expert_ids": expert_ids, "gate_values": gate_values, "gate_proj": gate_proj, "up_proj": up_proj, "down_proj": down_proj, "probe": probe}


def reference(tokens, cotangent, expert_ids, gate_values, gate_proj, up_proj, down_proj, probe):
    row_limit = N_DP * CAP
    gate_all = gate_proj.reshape(EXP_WIN, FF, D)
    up_all = up_proj.reshape(EXP_WIN, FF, D)
    down_all = down_proj.reshape(EXP_WIN, FF, D)
    probe_all = probe.reshape(EXP_WIN, FF, D)

    def per_expert(packed):
        expert, gate_rows, up_rows, down_rows, probe_rows = packed
        named = expert_ids == expert
        gate_sum = jnp.sum(jnp.where(named, gate_values, 0.0), axis=1)
        routed = jnp.any(named, axis=1)
        picked = jnp.nonzero(routed, size=row_limit, fill_value=0)[0].astype(jnp.int32)
        usable = jnp.arange(row_limit, dtype=jnp.int32) < jnp.sum(routed.astype(jnp.int32))
        rows_x = jnp.where(usable[:, None], tokens[picked], jnp.zeros((), tokens.dtype))
        factor = jnp.where(usable, gate_sum[picked], 0.0)
        rows_c = (factor[:, None] * cotangent[picked].astype(jnp.float32)).astype(jnp.bfloat16)
        preact = jnp.dot(rows_x, gate_rows.T, preferred_element_type=jnp.float32)
        linear = jnp.dot(rows_x, up_rows.T, preferred_element_type=jnp.float32)
        probe_pre = jnp.dot(rows_x, probe_rows.T, preferred_element_type=jnp.float32)
        backward = jnp.dot(rows_c, down_rows.T, preferred_element_type=jnp.float32)
        sigmoid_pre = jax.nn.sigmoid(preact)
        curvature = sigmoid_pre * (1.0 - sigmoid_pre) * (2.0 + preact * (1.0 - 2.0 * sigmoid_pre))
        tangent = (backward * linear * curvature * probe_pre).astype(jnp.bfloat16)
        return jnp.dot(tangent.T, rows_x, preferred_element_type=jnp.float32).astype(jnp.bfloat16)

    result = lax.map(per_expert, (jnp.arange(EXP_WIN, dtype=jnp.int32), gate_all, up_all, down_all, probe_all))
    return result.reshape(EXP_WIN * FF, D)
```

```python
import functools

import jax
import jax.numpy as jnp
from jax import lax
from jax.experimental import pallas as pl
from jax.experimental.pallas import tpu as pltpu
from jax.sharding import PartitionSpec as P

WIN = 4
CAP = 128
ZN, ZLO, ZHI = 32, 8, 4
F32, BF16 = jnp.float32, jnp.bfloat16
DPX = ("dp", "expert")
SMEM = pl.BlockSpec(memory_space=pltpu.SMEM)
VMEM = pl.BlockSpec(memory_space=pltpu.VMEM)


def dot(a, b):
    return jnp.dot(a, b, preferred_element_type=F32)


def prep_kernel(y_ref, ids_ref, gates_ref, tok_ref, cot_ref, send_ref, *rot_refs):
    y = y_ref[0]
    rows = tok_ref.shape[0]
    ids = ids_ref[...]
    gates = gates_ref[...]
    present, gate = [], []
    for j in range(WIN):
        named = ids == (y + j) % WIN
        present.append(jnp.max(jnp.where(named, 1.0, 0.0), axis=0, keepdims=True))
        gate.append(jnp.sum(jnp.where(named, gates, 0.0), axis=0, keepdims=True))
    marks = jnp.concatenate(present + present, axis=0)
    upper = (
        lax.broadcasted_iota(jnp.int32, (CAP, CAP), 0)
        <= lax.broadcasted_iota(jnp.int32, (CAP, CAP), 1)
    ).astype(BF16)
    base = jnp.full((2 * WIN, 1), -1.0, F32)
    slots = []
    for b in range(rows // CAP):
        part = dot(marks[:, b * CAP : (b + 1) * CAP].astype(BF16), upper)
        slots.append(part + base)
        base = base + part[:, CAP - 1 :]
    slot = jnp.concatenate(slots, axis=1)
    slot = jnp.where(marks > 0.0, slot, -1.0).astype(jnp.int32)
    both = jnp.concatenate([tok_ref[...], cot_ref[...]], axis=1)
    index = lax.broadcasted_iota(jnp.int32, (CAP, rows), 0)
    for j in range(WIN):
        placer = slot[j : j + 1, :] == index
        got = dot(jnp.where(placer, 1.0, 0.0).astype(BF16), both)
        factor = jnp.sum(jnp.where(placer, gate[j], 0.0), axis=1, keepdims=True)
        xs = got[:, :CAP]
        cs = got[:, CAP:] * factor
        rot_refs[j][...] = xs.astype(BF16)
        chunk = jnp.concatenate([xs.T, cs.T], axis=0).astype(BF16)
        for x in range(WIN):
            send_ref[((y + j) % WIN) * WIN + x] = chunk


def tangent_kernel(c_ref, own_ref, oth_ref, g_ref, u_ref, d_ref, p_ref, out_ref):
    c = c_ref[0]
    hid = g_ref.shape[0]
    accs = [jnp.zeros((hid, CAP), F32) for _ in range(4)]
    for s in range(0, 16, 2):
        for ref, side in ((own_ref, c), (oth_ref, 1 - c)):
            cols = [
                pl.ds(pl.multiple_of((2 * (s + t) + side) * CAP, CAP), CAP)
                for t in range(2)
            ]
            xs = jnp.concatenate([ref[s, :CAP], ref[s + 1, :CAP]], axis=0)
            cs = jnp.concatenate([ref[s, CAP:], ref[s + 1, CAP:]], axis=0)
            for n, (w_ref, rhs) in enumerate(
                ((g_ref, xs), (u_ref, xs), (p_ref, xs), (d_ref, cs))
            ):
                lhs = jnp.concatenate([w_ref[:, cols[0]], w_ref[:, cols[1]]], axis=1)
                accs[n] = accs[n] + dot(lhs, rhs)
    preact, linear, probe_pre, backward = accs
    sig = 1.0 / (1.0 + jnp.exp(-preact))
    curvature = sig * (1.0 - sig) * (2.0 + preact * (1.0 - 2.0 * sig))
    tangent = (backward * linear * curvature * probe_pre).astype(BF16)
    for i in range(ZLO):
        out_ref[i] = tangent


def outer_kernel(offsets, at_ref, tan_ref, own_ref, oth_ref, *out_refs):
    zhi, e, x, c = at_ref[0], at_ref[1], at_ref[2], at_ref[3]
    for m, out_ref in zip(offsets, out_refs, strict=True):
        j = (e - zhi - m + 2 * WIN) % WIN
        acc = None
        for dx in range(WIN):
            chip = (x - dx + WIN) % WIN
            lhs = jnp.concatenate(
                [tan_ref[2 * chip + c], tan_ref[2 * chip + 1 - c]], axis=1
            )
            rhs = jnp.concatenate([own_ref[dx, j], oth_ref[dx, j]], axis=0)
            part = dot(lhs, rhs)
            acc = part if acc is None else acc + part
        out_ref[...] = acc.astype(out_ref.dtype)


def call(kernel, out_shape, specs, flops, nbytes):
    return pl.pallas_call(
        kernel,
        out_shape=out_shape,
        in_specs=specs,
        out_specs=jax.tree.map(lambda _: VMEM, out_shape),
        compiler_params=pltpu.CompilerParams(vmem_limit_bytes=40 * 1024 * 1024),
        cost_estimate=pl.CostEstimate(
            flops=flops, bytes_accessed=nbytes, transcendentals=0
        ),
    )


def sds(shape, dtype):
    return jax.ShapeDtypeStruct(shape, dtype)


def on_device(tokens, cotangent, expert_ids, gate_values, gate_proj, up_proj, down_proj, probe):
    z, h = lax.axis_index("dp"), lax.axis_index("expert")
    zhi, e, x, c = z // ZLO, h // 8, (h // 2) % WIN, h % 2
    hid, feats = gate_proj.shape[0], tokens.shape[1]
    at = jnp.stack([zhi, e, x, c]).astype(jnp.int32)

    prepared = call(
        prep_kernel,
        [sds((16, 2 * feats, CAP), BF16)] + [sds((CAP, feats), BF16)] * WIN,
        [SMEM] + [VMEM] * 4,
        2 * 512 * 1024 * 256,
        2 << 20,
    )(at[1:2], expert_ids.T, gate_values.T, tokens, cotangent)
    send, rotated = prepared[0], prepared[1:]

    same_core = [[c0 + 2 * i for i in range(16)] for c0 in range(2)]
    own = lax.all_to_all(
        send, "expert", split_axis=0, concat_axis=0, tiled=True, axis_index_groups=same_core
    )
    swap = [(i, i ^ 1) for i in range(32)]
    oth = lax.ppermute(own, "expert", swap)

    moved = []
    for j in range(WIN):
        perm = [
            (i * 32 + k, (i // 8 * 8 + k % 8) * 32 + ((k // 8 + j) % 4) * 8 + i % 8)
            for i in range(ZN)
            for k in range(32)
        ]
        moved.append(lax.ppermute(rotated[j], DPX, perm))
    mine = jnp.stack(moved)
    ring = [mine]
    for dx in range(1, WIN):
        perm = [(k, k // 8 * 8 + (k // 2 % 4 + dx) % 4 * 2 + k % 2) for k in range(32)]
        ring.append(lax.ppermute(mine, "expert", perm))
    own_t = jnp.stack(ring)
    oth_t = lax.ppermute(own_t, "expert", swap)

    tangent = call(
        tangent_kernel,
        sds((ZLO, hid, CAP), BF16),
        [SMEM] + [VMEM] * 6,
        2 * 4 * hid * 4096 * CAP,
        9 << 20,
    )(at[3:4], own, oth, gate_proj, up_proj, down_proj, probe)
    near = [[8 * a + b for b in range(8)] for a in range(4)]
    tangents = lax.all_to_all(
        tangent, "dp", split_axis=0, concat_axis=0, tiled=True, axis_index_groups=near
    )

    def outer(offsets, dtype):
        return call(
            functools.partial(outer_kernel, offsets),
            [sds((hid, feats), dtype) for _ in offsets],
            [SMEM] + [VMEM] * 3,
            2 * len(offsets) * hid * 1024 * CAP,
            2 << 20,
        )(at, tangents, own_t, oth_t)

    def hop(value, by):
        return lax.ppermute(value, "dp", [(i, (i + by) % ZN) for i in range(ZN)])

    (far,) = outer((2,), BF16)
    half = hid // 2
    from_below, from_above = hop(far[:half], ZLO), hop(far[half:], -ZLO)
    here, up, down = outer((0, 1, 3), F32)
    up = jnp.concatenate([up[:half] + from_below.astype(F32), up[half:]]).astype(BF16)
    down = jnp.concatenate([down[:half], down[half:] + from_above.astype(F32)]).astype(BF16)
    total = here + hop(up, ZLO).astype(F32) + hop(down, -ZLO).astype(F32)
    return total.astype(BF16)


def solution(mesh):
    return jax.shard_map(
        on_device,
        mesh=mesh,
        in_specs=(
            P("dp", "expert"),
            P("dp", "expert"),
            P("dp", None),
            P("dp", None),
            P("expert", None),
            P("expert", None),
            P("expert", None),
            P("expert", None),
        ),
        out_specs=P("expert", "dp"),
        check_vma=False,
    )
```

```python
import functools

import jax
import jax.numpy as jnp
from jax import lax
from jax.experimental import pallas as pl
from jax.experimental.pallas import tpu as pltpu
from jax.sharding import PartitionSpec as P

WIN = 4
CAP = 128
ZN, ZLO, ZHI = 32, 8, 4
F32, BF16 = jnp.float32, jnp.bfloat16
DPX = ("dp", "expert")
SMEM = pl.BlockSpec(memory_space=pltpu.SMEM)
VMEM = pl.BlockSpec(memory_space=pltpu.VMEM)
ANY = pl.BlockSpec(memory_space=pl.ANY)
HBM = pl.BlockSpec(memory_space=pltpu.HBM)
DMA = pltpu.SemaphoreType.DMA


def dot(a, b):
    return jnp.dot(a, b, preferred_element_type=F32)


def prep_kernel(y_ref, ids_hbm, gates_hbm, tok_hbm, cot_hbm, send_ref, *refs):
    rot_refs, (ids_ref, gates_ref, both_ref, sems) = refs[:WIN], refs[WIN:]
    feats = tok_hbm.shape[1]
    copies = [
        pltpu.make_async_copy(ids_hbm, ids_ref, sems.at[0]),
        pltpu.make_async_copy(gates_hbm, gates_ref, sems.at[1]),
        pltpu.make_async_copy(tok_hbm, both_ref.at[:, pl.ds(0, feats)], sems.at[2]),
        pltpu.make_async_copy(cot_hbm, both_ref.at[:, pl.ds(feats, feats)], sems.at[3]),
    ]
    for copy in copies:
        copy.start()
    y = y_ref[0]
    rows = tok_hbm.shape[0]
    upper = (
        lax.broadcasted_iota(jnp.int32, (CAP, CAP), 0)
        <= lax.broadcasted_iota(jnp.int32, (CAP, CAP), 1)
    ).astype(BF16)
    copies[0].wait()
    copies[1].wait()
    ids = ids_ref[...]
    gates = gates_ref[...]
    present, gate = [], []
    for j in range(WIN):
        named = ids == (y + j) % WIN
        present.append(jnp.max(jnp.where(named, 1.0, 0.0), axis=0, keepdims=True))
        gate.append(jnp.sum(jnp.where(named, gates, 0.0), axis=0, keepdims=True))
    marks = jnp.concatenate(present + present, axis=0)
    base = jnp.full((2 * WIN, 1), -1.0, F32)
    slots = []
    for b in range(rows // CAP):
        part = dot(marks[:, b * CAP : (b + 1) * CAP].astype(BF16), upper)
        slots.append(part + base)
        base = base + part[:, CAP - 1 :]
    slot = jnp.concatenate(slots, axis=1)
    slot = jnp.where(marks > 0.0, slot, -1.0).astype(jnp.int32)
    index = lax.broadcasted_iota(jnp.int32, (CAP, rows), 0)
    copies[2].wait()
    copies[3].wait()
    both = both_ref[...]
    for j in range(WIN):
        placer = slot[j : j + 1, :] == index
        got = dot(jnp.where(placer, 1.0, 0.0).astype(BF16), both)
        factor = jnp.sum(jnp.where(placer, gate[j], 0.0), axis=1, keepdims=True)
        xs = got[:, :feats]
        cs = got[:, feats:] * factor
        rot_refs[j][...] = xs.astype(BF16)
        chunk = jnp.concatenate([xs.T, cs.T], axis=0).astype(BF16)
        for x in range(WIN):
            send_ref[((y + j) % WIN) * WIN + x] = chunk


def gate_kernel(rows_in, *refs):
    del rows_in
    moved_refs, mine_ref = refs[:WIN], refs[WIN + 1]
    for j in range(WIN):
        mine_ref[j] = moved_refs[j][...]


def load(side, w_hbms, w_ref, sem):
    for n, w_hbm in enumerate(w_hbms):
        for s in range(w_hbm.shape[1] // (2 * CAP)):
            cols = pl.ds(pl.multiple_of((2 * s + side) * CAP, CAP), CAP)
            dst = w_ref.at[n, :, pl.ds(s * CAP, CAP)]
            pltpu.make_async_copy(w_hbm.at[:, cols], dst, sem.at[n]).start()


def half(rows_ref, w_ref, sem):
    chips, both, slots = rows_ref.shape
    xs = rows_ref[:, : both // 2].reshape(chips * both // 2, slots)
    cs = rows_ref[:, both // 2 :].reshape(chips * both // 2, slots)
    parts = []
    for n, rows in enumerate((xs, xs, xs, cs)):
        pltpu.make_async_copy(w_ref.at[n], w_ref.at[n], sem.at[n]).wait()
        parts.append(dot(w_ref[n], rows))
    return parts


def own_kernel(c_ref, rows_ref, g_hbm, u_hbm, p_hbm, d_hbm, acc_ref, w_ref, sem):
    load(c_ref[0], (g_hbm, u_hbm, p_hbm, d_hbm), w_ref, sem)
    for n, part in enumerate(half(rows_ref, w_ref, sem)):
        acc_ref[n] = part


def tangent_kernel(c_ref, rows_ref, g_hbm, u_hbm, p_hbm, d_hbm, acc_ref, out_ref, w_ref, sem):
    load(1 - c_ref[0], (g_hbm, u_hbm, p_hbm, d_hbm), w_ref, sem)
    preact, linear, probe_pre, backward = [
        acc_ref[n] + part for n, part in enumerate(half(rows_ref, w_ref, sem))
    ]
    sig = 1.0 / (1.0 + jnp.exp(-preact))
    curvature = sig * (1.0 - sig) * (2.0 + preact * (1.0 - 2.0 * sig))
    tangent = (backward * linear * curvature * probe_pre).astype(BF16)
    for i in range(ZLO):
        out_ref[i] = tangent


def outer_kernel(offsets, at_ref, tan_ref, own_ref, oth_ref, *out_refs):
    zhi, e, x, c = at_ref[0], at_ref[1], at_ref[2], at_ref[3]
    for m, out_ref in zip(offsets, out_refs, strict=True):
        j = (e - zhi - m + 2 * WIN) % WIN
        acc = None
        for dx in range(WIN):
            chip = (x - dx + WIN) % WIN
            lhs = jnp.concatenate(
                [tan_ref[2 * chip + c], tan_ref[2 * chip + 1 - c]], axis=1
            )
            rhs = jnp.concatenate([own_ref[dx, j], oth_ref[dx, j]], axis=0)
            part = dot(lhs, rhs)
            acc = part if acc is None else acc + part
        out_ref[...] = acc.astype(out_ref.dtype)


def call(kernel, out_shape, specs, flops, nbytes, scratch=(), **more):
    return pl.pallas_call(
        kernel,
        out_shape=out_shape,
        in_specs=specs,
        scratch_shapes=scratch,
        compiler_params=pltpu.CompilerParams(vmem_limit_bytes=16 << 20),
        cost_estimate=pl.CostEstimate(
            flops=flops, bytes_accessed=nbytes, transcendentals=0
        ),
        **({"out_specs": jax.tree.map(lambda _: VMEM, out_shape)} | more),
    )


def in_hbm(value):
    return pltpu.with_memory_space_constraint(value, pltpu.HBM)


def sds(shape, dtype):
    return jax.ShapeDtypeStruct(shape, dtype)


def on_device(tokens, cotangent, expert_ids, gate_values, gate_proj, up_proj, down_proj, probe):
    z, h = lax.axis_index("dp"), lax.axis_index("expert")
    zhi, e, x, c = z // ZLO, h // 8, (h // 2) % WIN, h % 2
    hid, feats = gate_proj.shape[0], tokens.shape[1]
    at = jnp.stack([zhi, e, x, c]).astype(jnp.int32)

    rows, cols = tokens.shape[0], gate_proj.shape[1]
    send, *rotated = call(
        prep_kernel,
        [sds((16, 2 * feats, CAP), BF16)] + [sds((CAP, feats), BF16)] * WIN,
        [SMEM] + [HBM] * 4,
        2 * 512 * 1024 * 256,
        2 << 20,
        [
            pltpu.VMEM((8, rows), jnp.int32),
            pltpu.VMEM((8, rows), F32),
            pltpu.VMEM((rows, 2 * feats), BF16),
            DMA((4,)),
        ],
    )(at[1:2], *map(in_hbm, (expert_ids.T, gate_values.T, tokens, cotangent)))
    same_core = [[c0 + 2 * i for i in range(16)] for c0 in range(2)]
    own = lax.all_to_all(
        send, "expert", split_axis=0, concat_axis=0, tiled=True, axis_index_groups=same_core
    )
    moved = []
    for j in range(WIN):
        perm = [
            (i * 32 + k, (i // 8 * 8 + k % 8) * 32 + ((k // 8 + j) % 4) * 8 + i % 8)
            for i in range(ZN)
            for k in range(32)
        ]
        moved.append(lax.ppermute(rotated[j], DPX, perm))
    own, mine = call(
        gate_kernel,
        [sds(own.shape, BF16), sds((WIN, CAP, feats), BF16)],
        [ANY] + [VMEM] * WIN,
        0,
        1 << 18,
        out_specs=[ANY, VMEM],
        input_output_aliases={0: 0},
    )(own, *moved)
    swap = [(i, i ^ 1) for i in range(32)]
    oth = lax.ppermute(own, "expert", swap)

    weights = [in_hbm(w) for w in (gate_proj, up_proj, probe, down_proj)]
    columns = [pltpu.VMEM((4, hid, cols // 2), BF16), DMA((4,))]
    sums = call(
        own_kernel,
        sds((4, hid, CAP), F32),
        [SMEM, VMEM] + [HBM] * 4,
        4 * hid * cols * CAP,
        4 << 20,
        columns,
    )(at[3:4], own, *weights)
    tangent = call(
        tangent_kernel,
        sds((ZLO, hid, CAP), BF16),
        [SMEM, VMEM] + [HBM] * 4 + [VMEM],
        4 * hid * cols * CAP,
        4 << 20,
        columns,
    )(at[3:4], oth, *weights, sums)

    ring = [mine]
    for dx in range(1, WIN):
        perm = [(k, k // 8 * 8 + (k // 2 % 4 + dx) % 4 * 2 + k % 2) for k in range(32)]
        ring.append(lax.ppermute(mine, "expert", perm))
    own_t = jnp.stack(ring)
    oth_t = lax.ppermute(own_t, "expert", swap)

    near = [[8 * a + b for b in range(8)] for a in range(4)]
    tangents = lax.all_to_all(
        tangent, "dp", split_axis=0, concat_axis=0, tiled=True, axis_index_groups=near
    )

    def outer(offsets, dtype):
        return call(
            functools.partial(outer_kernel, offsets),
            [sds((hid, feats), dtype) for _ in offsets],
            [SMEM] + [VMEM] * 3,
            2 * len(offsets) * hid * 1024 * CAP,
            2 << 20,
        )(at, tangents, own_t, oth_t)

    def hop(value, by):
        return lax.ppermute(value, "dp", [(i, (i + by) % ZN) for i in range(ZN)])

    (far,) = outer((2,), BF16)
    half = hid // 2
    from_below, from_above = hop(far[:half], ZLO), hop(far[half:], -ZLO)
    here, up, down = outer((0, 1, 3), F32)
    up = jnp.concatenate([up[:half] + from_below.astype(F32), up[half:]]).astype(BF16)
    down = jnp.concatenate([down[:half], down[half:] + from_above.astype(F32)]).astype(BF16)
    total = here + hop(up, ZLO).astype(F32) + hop(down, -ZLO).astype(F32)
    return total.astype(BF16)


def solution(mesh):
    return jax.shard_map(
        on_device,
        mesh=mesh,
        in_specs=(
            P("dp", "expert"),
            P("dp", "expert"),
            P("dp", None),
            P("dp", None),
            P("expert", None),
            P("expert", None),
            P("expert", None),
            P("expert", None),
        ),
        out_specs=P("expert", "dp"),
        check_vma=False,
    )
```

```python
import jax
import jax.numpy as jnp
from jax import lax
from jax.experimental import pallas as pl
from jax.experimental.pallas import tpu as pltpu
from jax.sharding import PartitionSpec as P

WIN = 4
CAP = 128
ZN, ZLO, ZHI = 32, 8, 4
F32, BF16 = jnp.float32, jnp.bfloat16
DPX = ("dp", "expert")
SMEM = pl.BlockSpec(memory_space=pltpu.SMEM)
VMEM = pl.BlockSpec(memory_space=pltpu.VMEM)
ANY = pl.BlockSpec(memory_space=pl.ANY)
HBM = pl.BlockSpec(memory_space=pltpu.HBM)
DMA = pltpu.SemaphoreType.DMA


def dot(a, b):
    return jnp.dot(a, b, preferred_element_type=F32)


def prep_kernel(y_ref, ids_hbm, gates_hbm, tok_hbm, cot_hbm, send_ref, *refs):
    rot_refs, (ids_ref, gates_ref, both_ref, sems) = refs[:WIN], refs[WIN:]
    feats = tok_hbm.shape[1]
    copies = [
        pltpu.make_async_copy(ids_hbm, ids_ref, sems.at[0]),
        pltpu.make_async_copy(gates_hbm, gates_ref, sems.at[1]),
        pltpu.make_async_copy(tok_hbm, both_ref.at[:, pl.ds(0, feats)], sems.at[2]),
        pltpu.make_async_copy(cot_hbm, both_ref.at[:, pl.ds(feats, feats)], sems.at[3]),
    ]
    for copy in copies:
        copy.start()
    y = y_ref[0]
    rows = tok_hbm.shape[0]
    upper = (
        lax.broadcasted_iota(jnp.int32, (CAP, CAP), 0)
        <= lax.broadcasted_iota(jnp.int32, (CAP, CAP), 1)
    ).astype(BF16)
    copies[0].wait()
    copies[1].wait()
    ids = ids_ref[...]
    gates = gates_ref[...]
    present, gate = [], []
    for j in range(WIN):
        named = ids == (y + j) % WIN
        present.append(jnp.max(jnp.where(named, 1.0, 0.0), axis=0, keepdims=True))
        gate.append(jnp.sum(jnp.where(named, gates, 0.0), axis=0, keepdims=True))
    marks = jnp.concatenate(present + present, axis=0)
    base = jnp.full((2 * WIN, 1), -1.0, F32)
    slots = []
    for b in range(rows // CAP):
        part = dot(marks[:, b * CAP : (b + 1) * CAP].astype(BF16), upper)
        slots.append(part + base)
        base = base + part[:, CAP - 1 :]
    slot = jnp.concatenate(slots, axis=1)
    slot = jnp.where(marks > 0.0, slot, -1.0).astype(jnp.int32)
    index = lax.broadcasted_iota(jnp.int32, (CAP, rows), 0)
    copies[2].wait()
    copies[3].wait()
    both = both_ref[...]
    for j in range(WIN):
        placer = slot[j : j + 1, :] == index
        got = dot(jnp.where(placer, 1.0, 0.0).astype(BF16), both)
        factor = jnp.sum(jnp.where(placer, gate[j], 0.0), axis=1, keepdims=True)
        xs = got[:, :feats]
        cs = got[:, feats:] * factor
        rot_refs[j][...] = xs.astype(BF16)
        chunk = jnp.concatenate([xs.T, cs.T], axis=0).astype(BF16)
        for x in range(WIN):
            send_ref[((y + j) % WIN) * WIN + x] = chunk


def gate_kernel(rows_in, *refs):
    del rows_in
    moved_refs, mine_ref = refs[:WIN], refs[WIN + 1]
    for j in range(WIN):
        mine_ref[j] = moved_refs[j][...]


def load(side, w_hbms, w_ref, sem):
    for n, w_hbm in enumerate(w_hbms):
        for s in range(w_hbm.shape[1] // (2 * CAP)):
            cols = pl.ds(pl.multiple_of((2 * s + side) * CAP, CAP), CAP)
            dst = w_ref.at[n, :, pl.ds(s * CAP, CAP)]
            pltpu.make_async_copy(w_hbm.at[:, cols], dst, sem.at[n]).start()


def half(rows_ref, w_ref, sem):
    chips, both, slots = rows_ref.shape
    xs = rows_ref[:, : both // 2].reshape(chips * both // 2, slots)
    cs = rows_ref[:, both // 2 :].reshape(chips * both // 2, slots)
    parts = []
    for n, rows in enumerate((xs, xs, xs, cs)):
        pltpu.make_async_copy(w_ref.at[n], w_ref.at[n], sem.at[n]).wait()
        parts.append(dot(w_ref[n], rows))
    return parts


def own_kernel(c_ref, rows_ref, g_hbm, u_hbm, p_hbm, d_hbm, acc_ref, w_ref, sem):
    load(c_ref[0], (g_hbm, u_hbm, p_hbm, d_hbm), w_ref, sem)
    for n, part in enumerate(half(rows_ref, w_ref, sem)):
        acc_ref[n] = part


def tangent_kernel(c_ref, rows_ref, g_hbm, u_hbm, p_hbm, d_hbm, acc_ref, out_ref, w_ref, sem):
    load(1 - c_ref[0], (g_hbm, u_hbm, p_hbm, d_hbm), w_ref, sem)
    preact, linear, probe_pre, backward = [
        acc_ref[n] + part for n, part in enumerate(half(rows_ref, w_ref, sem))
    ]
    sig = 1.0 / (1.0 + jnp.exp(-preact))
    curvature = sig * (1.0 - sig) * (2.0 + preact * (1.0 - 2.0 * sig))
    tangent = (backward * linear * curvature * probe_pre).astype(BF16)
    for i in range(ZLO):
        out_ref[i] = tangent


def outer_kernel(at_ref, tan_ref, own_ref, oth_ref, out_ref):
    e, x, c = at_ref[0], at_ref[1], at_ref[2]
    for dest in range(ZHI):
        j = (e - dest + WIN) % WIN
        acc = None
        for dx in range(WIN):
            chip = (x - dx + WIN) % WIN
            lhs = jnp.concatenate(
                [tan_ref[2 * chip + c], tan_ref[2 * chip + 1 - c]], axis=1
            )
            rhs = jnp.concatenate([own_ref[dx, j], oth_ref[dx, j]], axis=0)
            part = dot(lhs, rhs)
            acc = part if acc is None else acc + part
        out_ref[dest] = acc.astype(out_ref.dtype)


def call(kernel, out_shape, specs, flops, nbytes, scratch=(), **more):
    return pl.pallas_call(
        kernel,
        out_shape=out_shape,
        in_specs=specs,
        scratch_shapes=scratch,
        compiler_params=pltpu.CompilerParams(vmem_limit_bytes=16 << 20),
        cost_estimate=pl.CostEstimate(
            flops=flops, bytes_accessed=nbytes, transcendentals=0
        ),
        **({"out_specs": jax.tree.map(lambda _: VMEM, out_shape)} | more),
    )


def in_hbm(value):
    return pltpu.with_memory_space_constraint(value, pltpu.HBM)


def sds(shape, dtype):
    return jax.ShapeDtypeStruct(shape, dtype)


def on_device(tokens, cotangent, expert_ids, gate_values, gate_proj, up_proj, down_proj, probe):
    h = lax.axis_index("expert")
    e, x, c = h // 8, (h // 2) % WIN, h % 2
    hid, feats = gate_proj.shape[0], tokens.shape[1]
    at = jnp.stack([e, x, c]).astype(jnp.int32)

    rows, cols = tokens.shape[0], gate_proj.shape[1]
    send, *rotated = call(
        prep_kernel,
        [sds((16, 2 * feats, CAP), BF16)] + [sds((CAP, feats), BF16)] * WIN,
        [SMEM] + [HBM] * 4,
        2 * 512 * 1024 * 256,
        2 << 20,
        [
            pltpu.VMEM((8, rows), jnp.int32),
            pltpu.VMEM((8, rows), F32),
            pltpu.VMEM((rows, 2 * feats), BF16),
            DMA((4,)),
        ],
    )(at[:1], *map(in_hbm, (expert_ids.T, gate_values.T, tokens, cotangent)))
    same_core = [[c0 + 2 * i for i in range(16)] for c0 in range(2)]
    own = lax.all_to_all(
        send, "expert", split_axis=0, concat_axis=0, tiled=True, axis_index_groups=same_core
    )
    moved = []
    for j in range(WIN):
        perm = [
            (i * 32 + k, (i // 8 * 8 + k % 8) * 32 + ((k // 8 + j) % 4) * 8 + i % 8)
            for i in range(ZN)
            for k in range(32)
        ]
        moved.append(lax.ppermute(rotated[j], DPX, perm))
    own, mine = call(
        gate_kernel,
        [sds(own.shape, BF16), sds((WIN, CAP, feats), BF16)],
        [ANY] + [VMEM] * WIN,
        0,
        1 << 18,
        out_specs=[ANY, VMEM],
        input_output_aliases={0: 0},
    )(own, *moved)
    swap = [(i, i ^ 1) for i in range(32)]
    oth = lax.ppermute(own, "expert", swap)

    weights = [in_hbm(w) for w in (gate_proj, up_proj, probe, down_proj)]
    columns = [pltpu.VMEM((4, hid, cols // 2), BF16), DMA((4,))]
    sums = call(
        own_kernel,
        sds((4, hid, CAP), F32),
        [SMEM, VMEM] + [HBM] * 4,
        4 * hid * cols * CAP,
        4 << 20,
        columns,
    )(at[2:], own, *weights)
    tangent = call(
        tangent_kernel,
        sds((ZLO, hid, CAP), BF16),
        [SMEM, VMEM] + [HBM] * 4 + [VMEM],
        4 * hid * cols * CAP,
        4 << 20,
        columns,
    )(at[2:], oth, *weights, sums)

    ring = [mine]
    for dx in range(1, WIN):
        perm = [(k, k // 8 * 8 + (k // 2 % 4 + dx) % 4 * 2 + k % 2) for k in range(32)]
        ring.append(lax.ppermute(mine, "expert", perm))
    own_t = jnp.stack(ring)
    oth_t = lax.ppermute(own_t, "expert", swap)

    near = [[8 * a + b for b in range(8)] for a in range(4)]
    tangents = lax.all_to_all(
        tangent, "dp", split_axis=0, concat_axis=0, tiled=True, axis_index_groups=near
    )

    partial = call(
        outer_kernel,
        sds((ZHI, hid, feats), BF16),
        [SMEM] + [VMEM] * 3,
        2 * ZHI * hid * 1024 * CAP,
        2 << 20,
    )(at, tangents, own_t, oth_t)
    far = [[8 * a + b for a in range(4)] for b in range(8)]
    parts = lax.all_to_all(
        partial, "dp", split_axis=0, concat_axis=0, tiled=True, axis_index_groups=far
    )
    return jnp.sum(parts.astype(F32), axis=0).astype(BF16)


def solution(mesh):
    return jax.shard_map(
        on_device,
        mesh=mesh,
        in_specs=(
            P("dp", "expert"),
            P("dp", "expert"),
            P("dp", None),
            P("dp", None),
            P("expert", None),
            P("expert", None),
            P("expert", None),
            P("expert", None),
        ),
        out_specs=P("expert", "dp"),
        check_vma=False,
    )
```

```python
import jax
import jax.numpy as jnp
from jax import lax
from jax.experimental import pallas as pl
from jax.experimental.pallas import tpu as pltpu
from jax.sharding import PartitionSpec as P

WIN = 4
CAP = 128
ZN, ZLO, ZHI = 32, 8, 4
F32, BF16 = jnp.float32, jnp.bfloat16
DPX = ("dp", "expert")
SMEM = pl.BlockSpec(memory_space=pltpu.SMEM)
VMEM = pl.BlockSpec(memory_space=pltpu.VMEM)
ANY = pl.BlockSpec(memory_space=pl.ANY)
HBM = pl.BlockSpec(memory_space=pltpu.HBM)
DMA = pltpu.SemaphoreType.DMA


def dot(a, b):
    return jnp.dot(a, b, preferred_element_type=F32)


def prep_kernel(ids_hbm, gates_hbm, tok_hbm, cot_hbm, sx_ref, sc_ref, ids_ref, gates_ref, both_ref, sems):
    feats = tok_hbm.shape[1]
    copies = [
        pltpu.make_async_copy(ids_hbm, ids_ref, sems.at[0]),
        pltpu.make_async_copy(gates_hbm, gates_ref, sems.at[1]),
        pltpu.make_async_copy(tok_hbm, both_ref.at[:, pl.ds(0, feats)], sems.at[2]),
        pltpu.make_async_copy(cot_hbm, both_ref.at[:, pl.ds(feats, feats)], sems.at[3]),
    ]
    for copy in copies:
        copy.start()
    rows = tok_hbm.shape[0]
    upper = (
        lax.broadcasted_iota(jnp.int32, (CAP, CAP), 0)
        <= lax.broadcasted_iota(jnp.int32, (CAP, CAP), 1)
    ).astype(BF16)
    copies[0].wait()
    copies[1].wait()
    ids = ids_ref[...]
    gates = gates_ref[...]
    present, gate = [], []
    for j in range(WIN):
        named = ids == j
        present.append(jnp.max(jnp.where(named, 1.0, 0.0), axis=0, keepdims=True))
        gate.append(jnp.sum(jnp.where(named, gates, 0.0), axis=0, keepdims=True))
    marks = jnp.concatenate(present + present, axis=0)
    base = jnp.full((2 * WIN, 1), -1.0, F32)
    slots = []
    for b in range(rows // CAP):
        part = dot(marks[:, b * CAP : (b + 1) * CAP].astype(BF16), upper)
        slots.append(part + base)
        base = base + part[:, CAP - 1 :]
    slot = jnp.concatenate(slots, axis=1)
    slot = jnp.where(marks > 0.0, slot, -1.0).astype(jnp.int32)
    index = lax.broadcasted_iota(jnp.int32, (CAP, rows), 0)
    copies[2].wait()
    copies[3].wait()
    both = both_ref[...]
    for j in range(WIN):
        placer = slot[j : j + 1, :] == index
        got = dot(jnp.where(placer, 1.0, 0.0).astype(BF16), both)
        factor = jnp.sum(jnp.where(placer, gate[j], 0.0), axis=1, keepdims=True)
        xs = got[:, :feats]
        cs = got[:, feats:] * factor
        xs = xs.T.astype(BF16)
        cs = cs.T.astype(BF16)
        for x in range(WIN):
            sx_ref[j * WIN + x] = xs
            sc_ref[j * WIN + x] = cs


def pick_kernel(at_ref, rows_ref, out_ref):
    for y in range(WIN):
        out_ref[y] = rows_ref[y * WIN + at_ref[0]]


def gate_kernel(rows_in, sums_in, moved_ref, rows_out, mine_ref):
    del rows_in, sums_in, rows_out
    mine_ref[...] = moved_ref[...]


def load(side, w_hbm, w_ref, sem):
    for s in range(w_hbm.shape[1] // (2 * CAP)):
        cols = pl.ds(pl.multiple_of((2 * s + side) * CAP, CAP), CAP)
        dst = w_ref.at[:, pl.ds(s * CAP, CAP)]
        pltpu.make_async_copy(w_hbm.at[:, cols], dst, sem).start()


def times(w_ref, sem, rows_ref):
    pltpu.make_async_copy(w_ref, w_ref, sem).wait()
    chips, feats, slots = rows_ref.shape
    return dot(w_ref[...], rows_ref[...].reshape(chips * feats, slots))


def project_kernel(c_ref, own_ref, oth_ref, g_hbm, u_hbm, p_hbm, out_ref, w_ref, sem):
    weights = (g_hbm, u_hbm, p_hbm)
    for n, w_hbm in enumerate(weights):
        for side, which in ((0, c_ref[0]), (1, 1 - c_ref[0])):
            load(which, w_hbm, w_ref.at[n, side], sem.at[n, side])
    for n in range(len(weights)):
        out_ref[n] = times(w_ref.at[n, 0], sem.at[n, 0], own_ref) + times(
            w_ref.at[n, 1], sem.at[n, 1], oth_ref
        )


def own_kernel(c_ref, rows_ref, d_hbm, acc_ref, rest_ref, w_ref, sem):
    load(c_ref[0], d_hbm, w_ref, sem.at[0])
    load(1 - c_ref[0], d_hbm, rest_ref, sem.at[1])
    acc_ref[...] = times(w_ref, sem.at[0], rows_ref)
    pltpu.make_async_copy(rest_ref, rest_ref, sem.at[1]).wait()


def tangent_kernel(rows_ref, w_ref, acc_ref, sums_ref, out_ref):
    chips, feats, slots = rows_ref.shape
    backward = acc_ref[...] + dot(w_ref[...], rows_ref[...].reshape(chips * feats, slots))
    preact, linear, probe_pre = sums_ref[0], sums_ref[1], sums_ref[2]
    sig = 1.0 / (1.0 + jnp.exp(-preact))
    curvature = sig * (1.0 - sig) * (2.0 + preact * (1.0 - 2.0 * sig))
    tangent = (backward * linear * curvature * probe_pre).astype(BF16)
    for i in range(ZLO):
        out_ref[i] = tangent


def outer_kernel(at_ref, tan_ref, own_ref, oth_ref, out_ref):
    x, c = at_ref[0], at_ref[1]
    for dest in range(ZHI):
        acc = None
        for dx in range(WIN):
            chip = (x - dx + WIN) % WIN
            lhs = jnp.concatenate(
                [tan_ref[2 * chip + c], tan_ref[2 * chip + 1 - c]], axis=1
            )
            rhs = jnp.concatenate([own_ref[dx, dest], oth_ref[dx, dest]], axis=1)
            part = lax.dot_general(
                lhs, rhs, (((1,), (1,)), ((), ())), preferred_element_type=F32
            )
            acc = part if acc is None else acc + part
        out_ref[dest] = acc.astype(out_ref.dtype)


def call(kernel, out_shape, specs, flops, nbytes, scratch=(), **more):
    return pl.pallas_call(
        kernel,
        out_shape=out_shape,
        in_specs=specs,
        scratch_shapes=scratch,
        compiler_params=pltpu.CompilerParams(vmem_limit_bytes=16 << 20),
        cost_estimate=pl.CostEstimate(
            flops=flops, bytes_accessed=nbytes, transcendentals=0
        ),
        **({"out_specs": jax.tree.map(lambda _: VMEM, out_shape)} | more),
    )


def in_hbm(value):
    return pltpu.with_memory_space_constraint(value, pltpu.HBM)


def sds(shape, dtype):
    return jax.ShapeDtypeStruct(shape, dtype)


def on_device(tokens, cotangent, expert_ids, gate_values, gate_proj, up_proj, down_proj, probe):
    z, h = lax.axis_index("dp"), lax.axis_index("expert")
    x, c = (h // 2) % WIN, h % 2
    hid, feats = gate_proj.shape[0], tokens.shape[1]
    at = jnp.stack([x, c, (x + z % ZLO // 2) % WIN]).astype(jnp.int32)
    rows, cols = tokens.shape[0], gate_proj.shape[1]
    sent = sds((16, feats, CAP), BF16)

    send_x, send_c = call(
        prep_kernel,
        [sent, sent],
        [HBM] * 4,
        2 * 512 * 1024 * 256,
        2 << 20,
        [
            pltpu.VMEM((8, rows), jnp.int32),
            pltpu.VMEM((8, rows), F32),
            pltpu.VMEM((rows, 2 * feats), BF16),
            DMA((4,)),
        ],
    )(*map(in_hbm, (expert_ids.T, gate_values.T, tokens, cotangent)))

    same_core = [[c0 + 2 * i for i in range(16)] for c0 in range(2)]
    swap = [(i, i ^ 1) for i in range(32)]

    def spread(send):
        return lax.all_to_all(
            send, "expert", split_axis=0, concat_axis=0, tiled=True, axis_index_groups=same_core
        )

    own_x, own_c = spread(send_x), spread(send_c)

    picked = call(
        pick_kernel, sds((WIN, feats, CAP), BF16), [SMEM, VMEM], 0, 1 << 18
    )(at[2:], own_x)
    perm = [
        (
            i * 32 + k,
            (i // 8 * 8 + (k // 2 % 4 + i % 8 // 2) % 4 * 2 + k % 2) * 32 + k // 8 * 8 + i % 8,
        )
        for i in range(ZN)
        for k in range(32)
    ]
    moved = lax.ppermute(picked, DPX, perm)

    oth_x = lax.ppermute(own_x, "expert", swap)
    weights = [in_hbm(w) for w in (gate_proj, up_proj, probe)]
    sums = call(
        project_kernel,
        sds((3, hid, CAP), F32),
        [SMEM, VMEM, VMEM] + [HBM] * 3,
        6 * hid * cols * CAP,
        6 << 20,
        [pltpu.VMEM((3, 2, hid, cols // 2), BF16), DMA((3, 2))],
    )(at[1:2], own_x, oth_x, *weights)
    own_c, mine = call(
        gate_kernel,
        [sent, sds((WIN, feats, CAP), BF16)],
        [ANY, ANY, VMEM],
        0,
        1 << 18,
        out_specs=[ANY, VMEM],
        input_output_aliases={0: 0},
    )(own_c, sums, moved)
    oth_c = lax.ppermute(own_c, "expert", swap)
    acc, rest = call(
        own_kernel,
        [sds((hid, CAP), F32), sds((hid, cols // 2), BF16)],
        [SMEM, VMEM, HBM],
        hid * cols * CAP,
        2 << 20,
        [pltpu.VMEM((hid, cols // 2), BF16), DMA((2,))],
    )(at[1:2], own_c, in_hbm(down_proj))
    tangent = call(
        tangent_kernel,
        sds((ZLO, hid, CAP), BF16),
        [VMEM] * 4,
        hid * cols * CAP,
        2 << 20,
    )(oth_c, rest, acc, sums)

    ring = [mine]
    for dx in range(1, WIN):
        perm = [(k, k // 8 * 8 + (k // 2 % 4 + dx) % 4 * 2 + k % 2) for k in range(32)]
        ring.append(lax.ppermute(mine, "expert", perm))
    own_t = jnp.stack(ring)
    oth_t = lax.ppermute(own_t, "expert", swap)

    near = [[8 * a + b for b in range(8)] for a in range(4)]
    tangents = lax.all_to_all(
        tangent, "dp", split_axis=0, concat_axis=0, tiled=True, axis_index_groups=near
    )

    partial = call(
        outer_kernel,
        sds((ZHI, hid, feats), BF16),
        [SMEM] + [VMEM] * 3,
        2 * ZHI * hid * 1024 * CAP,
        2 << 20,
    )(at[:2], tangents, own_t, oth_t)
    far = [[8 * a + b for a in range(4)] for b in range(8)]
    parts = lax.all_to_all(
        partial, "dp", split_axis=0, concat_axis=0, tiled=True, axis_index_groups=far
    )
    return jnp.sum(parts.astype(F32), axis=0).astype(BF16)


def solution(mesh):
    return jax.shard_map(
        on_device,
        mesh=mesh,
        in_specs=(
            P("dp", "expert"),
            P("dp", "expert"),
            P("dp", None),
            P("dp", None),
            P("expert", None),
            P("expert", None),
            P("expert", None),
            P("expert", None),
        ),
        out_specs=P("expert", "dp"),
        check_vma=False,
    )
```

```python
import jax
import jax.numpy as jnp
from jax import lax
from jax.experimental import pallas as pl
from jax.experimental.pallas import tpu as pltpu
from jax.sharding import PartitionSpec as P

WIN = 4
CAP = 128
ZN, ZLO, ZHI = 32, 8, 4
F32, BF16 = jnp.float32, jnp.bfloat16
DPX = ("dp", "expert")
SMEM = pl.BlockSpec(memory_space=pltpu.SMEM)
VMEM = pl.BlockSpec(memory_space=pltpu.VMEM)
HBM = pl.BlockSpec(memory_space=pltpu.HBM)
DMA = pltpu.SemaphoreType.DMA


def dot(a, b):
    return jnp.dot(a, b, preferred_element_type=F32)


def prep_kernel(ids_hbm, gates_hbm, tok_hbm, cot_hbm, send_ref, ids_ref, gates_ref, both_ref, sems):
    feats = tok_hbm.shape[1]
    copies = [
        pltpu.make_async_copy(ids_hbm, ids_ref, sems.at[0]),
        pltpu.make_async_copy(gates_hbm, gates_ref, sems.at[1]),
        pltpu.make_async_copy(tok_hbm, both_ref.at[:, pl.ds(0, feats)], sems.at[2]),
        pltpu.make_async_copy(cot_hbm, both_ref.at[:, pl.ds(feats, feats)], sems.at[3]),
    ]
    for copy in copies:
        copy.start()
    rows = tok_hbm.shape[0]
    upper = (
        lax.broadcasted_iota(jnp.int32, (CAP, CAP), 0)
        <= lax.broadcasted_iota(jnp.int32, (CAP, CAP), 1)
    ).astype(BF16)
    copies[0].wait()
    copies[1].wait()
    ids = ids_ref[...]
    gates = gates_ref[...]
    present, gate = [], []
    for j in range(WIN):
        named = ids == j
        present.append(jnp.max(jnp.where(named, 1.0, 0.0), axis=0, keepdims=True))
        gate.append(jnp.sum(jnp.where(named, gates, 0.0), axis=0, keepdims=True))
    marks = jnp.concatenate(present + present, axis=0)
    base = jnp.full((2 * WIN, 1), -1.0, F32)
    slots = []
    for b in range(rows // CAP):
        part = dot(marks[:, b * CAP : (b + 1) * CAP].astype(BF16), upper)
        slots.append(part + base)
        base = base + part[:, CAP - 1 :]
    slot = jnp.concatenate(slots, axis=1)
    slot = jnp.where(marks > 0.0, slot, -1.0).astype(jnp.int32)
    index = lax.broadcasted_iota(jnp.int32, (CAP, rows), 0)
    copies[2].wait()
    copies[3].wait()
    both = both_ref[...]
    for j in range(WIN):
        placer = slot[j : j + 1, :] == index
        got = dot(jnp.where(placer, 1.0, 0.0).astype(BF16), both)
        factor = jnp.sum(jnp.where(placer, gate[j], 0.0), axis=1, keepdims=True)
        xs = got[:, :feats]
        cs = got[:, feats:] * factor
        chunk = jnp.concatenate([xs.T, cs.T], axis=0).astype(BF16)
        for x in range(WIN):
            send_ref[j * WIN + x] = chunk


def pick_kernel(at_ref, rows_ref, out_ref):
    for y in range(WIN):
        out_ref[y] = rows_ref[y * WIN + at_ref[0], : out_ref.shape[1]]


def load(side, w_hbms, w_ref, sem):
    for n, w_hbm in enumerate(w_hbms):
        for s in range(w_hbm.shape[1] // (2 * CAP)):
            cols = pl.ds(pl.multiple_of((2 * s + side) * CAP, CAP), CAP)
            dst = w_ref.at[n, :, pl.ds(s * CAP, CAP)]
            pltpu.make_async_copy(w_hbm.at[:, cols], dst, sem.at[n]).start()


def half(rows_ref, w_ref, sem):
    chips, both, slots = rows_ref.shape
    xs = rows_ref[:, : both // 2].reshape(chips * both // 2, slots)
    cs = rows_ref[:, both // 2 :].reshape(chips * both // 2, slots)
    parts = []
    for n, rows in enumerate((xs, xs, xs, cs)):
        pltpu.make_async_copy(w_ref.at[n], w_ref.at[n], sem.at[n]).wait()
        parts.append(dot(w_ref[n], rows))
    return parts


def own_kernel(c_ref, rows_ref, g_hbm, u_hbm, p_hbm, d_hbm, acc_ref, w_ref, sem):
    load(c_ref[0], (g_hbm, u_hbm, p_hbm, d_hbm), w_ref, sem)
    for n, part in enumerate(half(rows_ref, w_ref, sem)):
        acc_ref[n] = part


def tangent_kernel(c_ref, rows_ref, g_hbm, u_hbm, p_hbm, d_hbm, acc_ref, out_ref, w_ref, sem):
    load(1 - c_ref[0], (g_hbm, u_hbm, p_hbm, d_hbm), w_ref, sem)
    preact, linear, probe_pre, backward = [
        acc_ref[n] + part for n, part in enumerate(half(rows_ref, w_ref, sem))
    ]
    sig = 1.0 / (1.0 + jnp.exp(-preact))
    curvature = sig * (1.0 - sig) * (2.0 + preact * (1.0 - 2.0 * sig))
    out_ref[...] = (backward * linear * curvature * probe_pre).astype(BF16)


def fan_kernel(tan_ref, moved_ref, out_ref, mine_ref):
    for i in range(ZLO):
        out_ref[i] = tan_ref[...]
    mine_ref[...] = moved_ref[...]


def outer_kernel(at_ref, tan_ref, own_ref, oth_ref, out_ref):
    x, c = at_ref[0], at_ref[1]
    for dest in range(ZHI):
        acc = None
        for dx in range(WIN):
            chip = (x - dx + WIN) % WIN
            lhs = jnp.concatenate(
                [tan_ref[2 * chip + c], tan_ref[2 * chip + 1 - c]], axis=1
            )
            rhs = jnp.concatenate([own_ref[dx, dest], oth_ref[dx, dest]], axis=1)
            part = lax.dot_general(
                lhs, rhs, (((1,), (1,)), ((), ())), preferred_element_type=F32
            )
            acc = part if acc is None else acc + part
        out_ref[dest] = acc.astype(out_ref.dtype)


def call(kernel, out_shape, specs, flops, nbytes, scratch=(), **more):
    return pl.pallas_call(
        kernel,
        out_shape=out_shape,
        in_specs=specs,
        scratch_shapes=scratch,
        compiler_params=pltpu.CompilerParams(vmem_limit_bytes=16 << 20),
        cost_estimate=pl.CostEstimate(
            flops=flops, bytes_accessed=nbytes, transcendentals=0
        ),
        **({"out_specs": jax.tree.map(lambda _: VMEM, out_shape)} | more),
    )


def in_hbm(value):
    return pltpu.with_memory_space_constraint(value, pltpu.HBM)


def sds(shape, dtype):
    return jax.ShapeDtypeStruct(shape, dtype)


def on_device(tokens, cotangent, expert_ids, gate_values, gate_proj, up_proj, down_proj, probe):
    z, h = lax.axis_index("dp"), lax.axis_index("expert")
    x, c = (h // 2) % WIN, h % 2
    hid, feats = gate_proj.shape[0], tokens.shape[1]
    at = jnp.stack([x, c, (x + z % ZLO // 2 + z % 2 + 2 * c) % WIN]).astype(jnp.int32)
    rows, cols = tokens.shape[0], gate_proj.shape[1]

    send = call(
        prep_kernel,
        sds((16, 2 * feats, CAP), BF16),
        [HBM] * 4,
        2 * 512 * 1024 * 256,
        2 << 20,
        [
            pltpu.VMEM((8, rows), jnp.int32),
            pltpu.VMEM((8, rows), F32),
            pltpu.VMEM((rows, 2 * feats), BF16),
            DMA((4,)),
        ],
    )(*map(in_hbm, (expert_ids.T, gate_values.T, tokens, cotangent)))

    same_core = [[c0 + 2 * i for i in range(16)] for c0 in range(2)]
    own = lax.all_to_all(
        send, "expert", split_axis=0, concat_axis=0, tiled=True, axis_index_groups=same_core
    )
    swap = [(i, i ^ 1) for i in range(32)]
    oth = lax.ppermute(own, "expert", swap)

    picked = call(
        pick_kernel, sds((WIN, feats, CAP), BF16), [SMEM, VMEM], 0, 1 << 18
    )(at[2:], own)
    perm = [
        (
            i * 32 + k,
            (i // 8 * 8 + (k // 2 + i % 8 // 2 + i % 2 + 2 * (k % 2)) % 4 * 2 + k % 2) * 32 + k // 8 * 8 + i % 8,
        )
        for i in range(ZN)
        for k in range(32)
    ]
    moved = lax.ppermute(picked, DPX, perm)

    weights = [in_hbm(w) for w in (gate_proj, up_proj, probe, down_proj)]
    columns = [pltpu.VMEM((4, hid, cols // 2), BF16), DMA((4,))]
    sums = call(
        own_kernel,
        sds((4, hid, CAP), F32),
        [SMEM, VMEM] + [HBM] * 4,
        4 * hid * cols * CAP,
        4 << 20,
        columns,
    )(at[1:2], own, *weights)
    tangent = call(
        tangent_kernel,
        sds((hid, CAP), BF16),
        [SMEM, VMEM] + [HBM] * 4 + [VMEM],
        4 * hid * cols * CAP,
        4 << 20,
        columns,
    )(at[1:2], oth, *weights, sums)

    tangent, mine = call(
        fan_kernel,
        [sds((ZLO, hid, CAP), BF16), sds((WIN, feats, CAP), BF16)],
        [VMEM, VMEM],
        0,
        1 << 19,
    )(tangent, moved)

    ring = [mine]
    for dx in range(1, WIN):
        perm = [(k, k // 8 * 8 + (k // 2 % 4 + dx) % 4 * 2 + k % 2) for k in range(32)]
        ring.append(lax.ppermute(mine, "expert", perm))
    own_t = jnp.stack(ring)
    oth_t = lax.ppermute(own_t, "expert", swap)

    near = [[8 * a + b for b in range(8)] for a in range(4)]
    tangents = lax.all_to_all(
        tangent, "dp", split_axis=0, concat_axis=0, tiled=True, axis_index_groups=near
    )

    partial = call(
        outer_kernel,
        sds((ZHI, hid, feats), BF16),
        [SMEM] + [VMEM] * 3,
        2 * ZHI * hid * 1024 * CAP,
        2 << 20,
    )(at[:2], tangents, own_t, oth_t)
    far = [[8 * a + b for a in range(4)] for b in range(8)]
    parts = lax.all_to_all(
        partial, "dp", split_axis=0, concat_axis=0, tiled=True, axis_index_groups=far
    )
    return jnp.sum(parts.astype(F32), axis=0).astype(BF16)


def solution(mesh):
    return jax.shard_map(
        on_device,
        mesh=mesh,
        in_specs=(
            P("dp", "expert"),
            P("dp", "expert"),
            P("dp", None),
            P("dp", None),
            P("expert", None),
            P("expert", None),
            P("expert", None),
            P("expert", None),
        ),
        out_specs=P("expert", "dp"),
        check_vma=False,
    )
```

```python
import jax
import jax.numpy as jnp
from jax import lax
from jax.experimental import pallas as pl
from jax.experimental.pallas import tpu as pltpu
from jax.sharding import PartitionSpec as P

WIN = 4
CAP = 128
ZN, ZLO, ZHI = 32, 8, 4
F32, BF16 = jnp.float32, jnp.bfloat16
DPX = ("dp", "expert")
PAIRS = ((0, 2), (2, 3), (0, 3), (1, 2), (1, 3), (0, 1))
SMEM = pl.BlockSpec(memory_space=pltpu.SMEM)
VMEM = pl.BlockSpec(memory_space=pltpu.VMEM)
HBM = pl.BlockSpec(memory_space=pltpu.HBM)
DMA = pltpu.SemaphoreType.DMA


def dot(a, b):
    return jnp.dot(a, b, preferred_element_type=F32)


def prep_kernel(ids_hbm, gates_hbm, tok_hbm, cot_hbm, send_ref, ids_ref, gates_ref, both_ref, sems):
    feats = tok_hbm.shape[1]
    copies = [
        pltpu.make_async_copy(ids_hbm, ids_ref, sems.at[0]),
        pltpu.make_async_copy(gates_hbm, gates_ref, sems.at[1]),
        pltpu.make_async_copy(tok_hbm, both_ref.at[:, pl.ds(0, feats)], sems.at[2]),
        pltpu.make_async_copy(cot_hbm, both_ref.at[:, pl.ds(feats, feats)], sems.at[3]),
    ]
    for copy in copies:
        copy.start()
    rows = tok_hbm.shape[0]
    upper = (
        lax.broadcasted_iota(jnp.int32, (CAP, CAP), 0)
        <= lax.broadcasted_iota(jnp.int32, (CAP, CAP), 1)
    ).astype(BF16)
    copies[0].wait()
    copies[1].wait()
    ids = ids_ref[...]
    gates = gates_ref[...]
    present, gate = [], []
    for j in range(WIN):
        named = ids == j
        present.append(jnp.max(jnp.where(named, 1.0, 0.0), axis=0, keepdims=True))
        gate.append(jnp.sum(jnp.where(named, gates, 0.0), axis=0, keepdims=True))
    marks = jnp.concatenate(present + present, axis=0)
    base = jnp.full((2 * WIN, 1), -1.0, F32)
    slots = []
    for b in range(rows // CAP):
        part = dot(marks[:, b * CAP : (b + 1) * CAP].astype(BF16), upper)
        slots.append(part + base)
        base = base + part[:, CAP - 1 :]
    slot = jnp.concatenate(slots, axis=1)
    slot = jnp.where(marks > 0.0, slot, -1.0).astype(jnp.int32)
    index = lax.broadcasted_iota(jnp.int32, (CAP, rows), 0)
    copies[2].wait()
    copies[3].wait()
    both = both_ref[...]
    for j in range(WIN):
        placer = slot[j : j + 1, :] == index
        got = dot(jnp.where(placer, 1.0, 0.0).astype(BF16), both)
        factor = jnp.sum(jnp.where(placer, gate[j], 0.0), axis=1, keepdims=True)
        xs = got[:, :feats]
        cs = got[:, feats:] * factor
        chunk = jnp.concatenate([xs.T, cs.T], axis=0).astype(BF16)
        for x in range(WIN):
            send_ref[j * WIN + x] = chunk


def pick_kernel(at_ref, rows_ref, out_ref):
    for y in range(WIN):
        out_ref[y] = rows_ref[y * WIN + at_ref[0], : out_ref.shape[1]]


def load(side, w_hbms, w_ref, sem):
    for n, w_hbm in enumerate(w_hbms):
        for s in range(w_hbm.shape[1] // (2 * CAP)):
            cols = pl.ds(pl.multiple_of((2 * s + side) * CAP, CAP), CAP)
            dst = w_ref.at[n, :, pl.ds(s * CAP, CAP)]
            pltpu.make_async_copy(w_hbm.at[:, cols], dst, sem.at[n]).start()


def half(rows_ref, w_ref, sem):
    chips, both, slots = rows_ref.shape
    xs = rows_ref[:, : both // 2].reshape(chips * both // 2, slots)
    cs = rows_ref[:, both // 2 :].reshape(chips * both // 2, slots)
    parts = []
    for n, rows in enumerate((xs, xs, xs, cs)):
        pltpu.make_async_copy(w_ref.at[n], w_ref.at[n], sem.at[n]).wait()
        parts.append(dot(w_ref[n], rows))
    return parts


def own_kernel(c_ref, rows_ref, g_hbm, u_hbm, p_hbm, d_hbm, acc_ref, w_ref, sem):
    load(c_ref[0], (g_hbm, u_hbm, p_hbm, d_hbm), w_ref, sem)
    for n, part in enumerate(half(rows_ref, w_ref, sem)):
        acc_ref[n] = part


def tangent_kernel(c_ref, rows_ref, g_hbm, u_hbm, p_hbm, d_hbm, acc_ref, out_ref, w_ref, sem):
    load(1 - c_ref[0], (g_hbm, u_hbm, p_hbm, d_hbm), w_ref, sem)
    preact, linear, probe_pre, backward = [
        acc_ref[n] + part for n, part in enumerate(half(rows_ref, w_ref, sem))
    ]
    sig = 1.0 / (1.0 + jnp.exp(-preact))
    curvature = sig * (1.0 - sig) * (2.0 + preact * (1.0 - 2.0 * sig))
    out_ref[...] = (backward * linear * curvature * probe_pre).astype(BF16)


def fan_kernel(tan_ref, moved_ref, out_ref, mine_ref):
    for i in range(ZLO):
        out_ref[i] = tan_ref[...]
    mine_ref[...] = moved_ref[...]


def outer_kernel(at_ref, tan_ref, own_ref, oth_ref, *out_refs):
    x, c, zhi = at_ref[0], at_ref[1], at_ref[2]
    for dest, out_ref in zip((zhi, *others(zhi)), out_refs, strict=True):
        acc = None
        for dx in range(WIN):
            chip = (x - dx + WIN) % WIN
            lhs = jnp.concatenate(
                [tan_ref[2 * chip + c], tan_ref[2 * chip + 1 - c]], axis=1
            )
            rhs = jnp.concatenate([own_ref[dx, dest], oth_ref[dx, dest]], axis=1)
            part = lax.dot_general(
                lhs, rhs, (((1,), (1,)), ((), ())), preferred_element_type=F32
            )
            acc = part if acc is None else acc + part
        out_ref[...] = acc.astype(out_ref.dtype)


def others(zhi):
    low = zhi % 2
    return zhi + 1 - 2 * low, (zhi + 2) % ZHI, 3 - zhi


def call(kernel, out_shape, specs, flops, nbytes, scratch=(), **more):
    return pl.pallas_call(
        kernel,
        out_shape=out_shape,
        in_specs=specs,
        scratch_shapes=scratch,
        compiler_params=pltpu.CompilerParams(vmem_limit_bytes=16 << 20),
        cost_estimate=pl.CostEstimate(
            flops=flops, bytes_accessed=nbytes, transcendentals=0
        ),
        **({"out_specs": jax.tree.map(lambda _: VMEM, out_shape)} | more),
    )


def in_hbm(value):
    return pltpu.with_memory_space_constraint(value, pltpu.HBM)


def sds(shape, dtype):
    return jax.ShapeDtypeStruct(shape, dtype)


def on_device(tokens, cotangent, expert_ids, gate_values, gate_proj, up_proj, down_proj, probe):
    z, h = lax.axis_index("dp"), lax.axis_index("expert")
    x, c = (h // 2) % WIN, h % 2
    hid, feats = gate_proj.shape[0], tokens.shape[1]
    at = jnp.stack([x, c, z // ZLO, (x + z % ZLO // 2 + z % 2 + 2 * c) % WIN]).astype(jnp.int32)
    rows, cols = tokens.shape[0], gate_proj.shape[1]

    send = call(
        prep_kernel,
        sds((16, 2 * feats, CAP), BF16),
        [HBM] * 4,
        2 * 512 * 1024 * 256,
        2 << 20,
        [
            pltpu.VMEM((8, rows), jnp.int32),
            pltpu.VMEM((8, rows), F32),
            pltpu.VMEM((rows, 2 * feats), BF16),
            DMA((4,)),
        ],
    )(*map(in_hbm, (expert_ids.T, gate_values.T, tokens, cotangent)))

    same_core = [[c0 + 2 * i for i in range(16)] for c0 in range(2)]
    own = lax.all_to_all(
        send, "expert", split_axis=0, concat_axis=0, tiled=True, axis_index_groups=same_core
    )
    swap = [(i, i ^ 1) for i in range(32)]
    oth = lax.ppermute(own, "expert", swap)

    picked = call(
        pick_kernel, sds((WIN, feats, CAP), BF16), [SMEM, VMEM], 0, 1 << 18
    )(at[3:], own)
    perm = [
        (
            i * 32 + k,
            (i // 8 * 8 + (k // 2 + i % 8 // 2 + i % 2 + 2 * (k % 2)) % 4 * 2 + k % 2) * 32 + k // 8 * 8 + i % 8,
        )
        for i in range(ZN)
        for k in range(32)
    ]
    moved = lax.ppermute(picked, DPX, perm)

    weights = [in_hbm(w) for w in (gate_proj, up_proj, probe, down_proj)]
    columns = [pltpu.VMEM((4, hid, cols // 2), BF16), DMA((4,))]
    sums = call(
        own_kernel,
        sds((4, hid, CAP), F32),
        [SMEM, VMEM] + [HBM] * 4,
        4 * hid * cols * CAP,
        4 << 20,
        columns,
    )(at[1:2], own, *weights)
    tangent = call(
        tangent_kernel,
        sds((hid, CAP), BF16),
        [SMEM, VMEM] + [HBM] * 4 + [VMEM],
        4 * hid * cols * CAP,
        4 << 20,
        columns,
    )(at[1:2], oth, *weights, sums)

    tangent, mine = call(
        fan_kernel,
        [sds((ZLO, hid, CAP), BF16), sds((WIN, feats, CAP), BF16)],
        [VMEM, VMEM],
        0,
        1 << 19,
    )(tangent, moved)

    ring = [mine]
    for dx in range(1, WIN):
        perm = [(k, k // 8 * 8 + (k // 2 % 4 + dx) % 4 * 2 + k % 2) for k in range(32)]
        ring.append(lax.ppermute(mine, "expert", perm))
    own_t = jnp.stack(ring)
    oth_t = lax.ppermute(own_t, "expert", swap)

    near = [[8 * a + b for b in range(8)] for a in range(4)]
    tangents = lax.all_to_all(
        tangent, "dp", split_axis=0, concat_axis=0, tiled=True, axis_index_groups=near
    )

    here, *away = call(
        outer_kernel,
        [sds((hid, feats), F32)] + [sds((hid, feats), BF16)] * 3,
        [SMEM] + [VMEM] * 3,
        2 * ZHI * hid * 1024 * CAP,
        2 << 20,
    )(at[:3], tangents, own_t, oth_t)
    total = here
    for a, b in PAIRS:
        perm = [(8 * s + i, 8 * d + i) for s, d in ((a, b), (b, a)) for i in range(ZLO)]
        total = total + lax.ppermute(away[(a ^ b) - 1], "dp", perm).astype(F32)
    return total.astype(BF16)


def solution(mesh):
    return jax.shard_map(
        on_device,
        mesh=mesh,
        in_specs=(
            P("dp", "expert"),
            P("dp", "expert"),
            P("dp", None),
            P("dp", None),
            P("expert", None),
            P("expert", None),
            P("expert", None),
            P("expert", None),
        ),
        out_specs=P("expert", "dp"),
        check_vma=False,
    )
```

```python
import functools

import jax
import jax.numpy as jnp
from jax import lax
from jax.experimental import pallas as pl
from jax.experimental.pallas import tpu as pltpu
from jax.sharding import PartitionSpec as P

WIN = 4
CAP = 128
ZN, ZLO, ZHI = 32, 8, 4
F32, BF16 = jnp.float32, jnp.bfloat16
DPX = ("dp", "expert")
SMEM = pl.BlockSpec(memory_space=pltpu.SMEM)
VMEM = pl.BlockSpec(memory_space=pltpu.VMEM)
HBM = pl.BlockSpec(memory_space=pltpu.HBM)
DMA = pltpu.SemaphoreType.DMA


def dot(a, b):
    return jnp.dot(a, b, preferred_element_type=F32)


def prep_kernel(ids_hbm, gates_hbm, tok_hbm, cot_hbm, send_ref, ids_ref, gates_ref, both_ref, sems):
    feats = tok_hbm.shape[1]
    copies = [
        pltpu.make_async_copy(ids_hbm, ids_ref, sems.at[0]),
        pltpu.make_async_copy(gates_hbm, gates_ref, sems.at[1]),
        pltpu.make_async_copy(tok_hbm, both_ref.at[:, pl.ds(0, feats)], sems.at[2]),
        pltpu.make_async_copy(cot_hbm, both_ref.at[:, pl.ds(feats, feats)], sems.at[3]),
    ]
    for copy in copies:
        copy.start()
    rows = tok_hbm.shape[0]
    upper = (
        lax.broadcasted_iota(jnp.int32, (CAP, CAP), 0)
        <= lax.broadcasted_iota(jnp.int32, (CAP, CAP), 1)
    ).astype(BF16)
    copies[0].wait()
    copies[1].wait()
    ids = ids_ref[...]
    gates = gates_ref[...]
    present, gate = [], []
    for j in range(WIN):
        named = ids == j
        present.append(jnp.max(jnp.where(named, 1.0, 0.0), axis=0, keepdims=True))
        gate.append(jnp.sum(jnp.where(named, gates, 0.0), axis=0, keepdims=True))
    marks = jnp.concatenate(present + present, axis=0)
    base = jnp.full((2 * WIN, 1), -1.0, F32)
    slots = []
    for b in range(rows // CAP):
        part = dot(marks[:, b * CAP : (b + 1) * CAP].astype(BF16), upper)
        slots.append(part + base)
        base = base + part[:, CAP - 1 :]
    slot = jnp.concatenate(slots, axis=1)
    slot = jnp.where(marks > 0.0, slot, -1.0).astype(jnp.int32)
    index = lax.broadcasted_iota(jnp.int32, (CAP, rows), 0)
    copies[2].wait()
    copies[3].wait()
    both = both_ref[...]
    for j in range(WIN):
        placer = slot[j : j + 1, :] == index
        got = dot(jnp.where(placer, 1.0, 0.0).astype(BF16), both)
        factor = jnp.sum(jnp.where(placer, gate[j], 0.0), axis=1, keepdims=True)
        xs = got[:, :feats]
        cs = got[:, feats:] * factor
        chunk = jnp.concatenate([xs.T, cs.T], axis=0).astype(BF16)
        for x in range(WIN):
            send_ref[j * WIN + x] = chunk


def pick_kernel(at_ref, rows_ref, out_ref):
    for y in range(WIN):
        out_ref[y] = rows_ref[y * WIN + at_ref[0], : out_ref.shape[1]]


def load(side, w_hbms, w_ref, sem):
    for n, w_hbm in enumerate(w_hbms):
        for s in range(w_hbm.shape[1] // (2 * CAP)):
            cols = pl.ds(pl.multiple_of((2 * s + side) * CAP, CAP), CAP)
            dst = w_ref.at[n, :, pl.ds(s * CAP, CAP)]
            pltpu.make_async_copy(w_hbm.at[:, cols], dst, sem.at[n]).start()


def half(rows_ref, w_ref, sem):
    chips, both, slots = rows_ref.shape
    xs = rows_ref[:, : both // 2].reshape(chips * both // 2, slots)
    cs = rows_ref[:, both // 2 :].reshape(chips * both // 2, slots)
    parts = []
    for n, rows in enumerate((xs, xs, xs, cs)):
        pltpu.make_async_copy(w_ref.at[n], w_ref.at[n], sem.at[n]).wait()
        parts.append(dot(w_ref[n], rows))
    return parts


def own_kernel(c_ref, rows_ref, g_hbm, u_hbm, p_hbm, d_hbm, acc_ref, w_ref, sem):
    load(c_ref[0], (g_hbm, u_hbm, p_hbm, d_hbm), w_ref, sem)
    for n, part in enumerate(half(rows_ref, w_ref, sem)):
        acc_ref[n] = part


def tangent_kernel(c_ref, rows_ref, g_hbm, u_hbm, p_hbm, d_hbm, acc_ref, out_ref, w_ref, sem):
    load(1 - c_ref[0], (g_hbm, u_hbm, p_hbm, d_hbm), w_ref, sem)
    preact, linear, probe_pre, backward = [
        acc_ref[n] + part for n, part in enumerate(half(rows_ref, w_ref, sem))
    ]
    sig = 1.0 / (1.0 + jnp.exp(-preact))
    curvature = sig * (1.0 - sig) * (2.0 + preact * (1.0 - 2.0 * sig))
    out_ref[...] = (backward * linear * curvature * probe_pre).astype(BF16)


def fan_kernel(tan_ref, moved_ref, out_ref, mine_ref):
    for i in range(ZLO):
        out_ref[i] = tan_ref[...]
    mine_ref[...] = moved_ref[...]


def outer_kernel(flips, at_ref, tan_ref, own_ref, oth_ref, out_ref):
    x, c, zhi = at_ref[0], at_ref[1], at_ref[2]
    for n, flip in enumerate(flips):
        dest = flipped(zhi, flip, c)
        acc = None
        for dx in range(WIN):
            chip = (x - dx + WIN) % WIN
            lhs = jnp.concatenate(
                [tan_ref[2 * chip + c], tan_ref[2 * chip + 1 - c]], axis=1
            )
            rhs = jnp.concatenate([own_ref[dx, dest], oth_ref[dx, dest]], axis=1)
            part = lax.dot_general(
                lhs, rhs, (((1,), (1,)), ((), ())), preferred_element_type=F32
            )
            acc = part if acc is None else acc + part
        out_ref[n] = acc.astype(out_ref.dtype)


def flipped(zhi, flip, core):
    near, mirror = zhi + 1 - 2 * (zhi % 2), 3 - zhi
    first = near + core * (mirror - near)
    return (zhi, first, near + mirror - first, (zhi + 2) % ZHI)[flip]


def call(kernel, out_shape, specs, flops, nbytes, scratch=(), **more):
    return pl.pallas_call(
        kernel,
        out_shape=out_shape,
        in_specs=specs,
        scratch_shapes=scratch,
        compiler_params=pltpu.CompilerParams(vmem_limit_bytes=16 << 20),
        cost_estimate=pl.CostEstimate(
            flops=flops, bytes_accessed=nbytes, transcendentals=0
        ),
        **({"out_specs": jax.tree.map(lambda _: VMEM, out_shape)} | more),
    )


def in_hbm(value):
    return pltpu.with_memory_space_constraint(value, pltpu.HBM)


def sds(shape, dtype):
    return jax.ShapeDtypeStruct(shape, dtype)


def on_device(tokens, cotangent, expert_ids, gate_values, gate_proj, up_proj, down_proj, probe):
    z, h = lax.axis_index("dp"), lax.axis_index("expert")
    x, c = (h // 2) % WIN, h % 2
    hid, feats = gate_proj.shape[0], tokens.shape[1]
    at = jnp.stack([x, c, z // ZLO, (x + z % ZLO // 2 + z % 2 + 2 * c) % WIN]).astype(jnp.int32)
    rows, cols = tokens.shape[0], gate_proj.shape[1]

    send = call(
        prep_kernel,
        sds((16, 2 * feats, CAP), BF16),
        [HBM] * 4,
        2 * 512 * 1024 * 256,
        2 << 20,
        [
            pltpu.VMEM((8, rows), jnp.int32),
            pltpu.VMEM((8, rows), F32),
            pltpu.VMEM((rows, 2 * feats), BF16),
            DMA((4,)),
        ],
    )(*map(in_hbm, (expert_ids.T, gate_values.T, tokens, cotangent)))

    same_core = [[c0 + 2 * i for i in range(16)] for c0 in range(2)]
    own = lax.all_to_all(
        send, "expert", split_axis=0, concat_axis=0, tiled=True, axis_index_groups=same_core
    )
    swap = [(i, i ^ 1) for i in range(32)]
    oth = lax.ppermute(own, "expert", swap)

    picked = call(
        pick_kernel, sds((WIN, feats, CAP), BF16), [SMEM, VMEM], 0, 1 << 18
    )(at[3:], own)
    perm = [
        (
            i * 32 + k,
            (i // 8 * 8 + (k // 2 + i % 8 // 2 + i % 2 + 2 * (k % 2)) % 4 * 2 + k % 2) * 32 + k // 8 * 8 + i % 8,
        )
        for i in range(ZN)
        for k in range(32)
    ]
    moved = lax.ppermute(picked, DPX, perm)

    weights = [in_hbm(w) for w in (gate_proj, up_proj, probe, down_proj)]
    columns = [pltpu.VMEM((4, hid, cols // 2), BF16), DMA((4,))]
    sums = call(
        own_kernel,
        sds((4, hid, CAP), F32),
        [SMEM, VMEM] + [HBM] * 4,
        4 * hid * cols * CAP,
        4 << 20,
        columns,
    )(at[1:2], own, *weights)
    tangent = call(
        tangent_kernel,
        sds((hid, CAP), BF16),
        [SMEM, VMEM] + [HBM] * 4 + [VMEM],
        4 * hid * cols * CAP,
        4 << 20,
        columns,
    )(at[1:2], oth, *weights, sums)

    tangent, mine = call(
        fan_kernel,
        [sds((ZLO, hid, CAP), BF16), sds((WIN, feats, CAP), BF16)],
        [VMEM, VMEM],
        0,
        1 << 19,
    )(tangent, moved)

    ring = [mine]
    for dx in range(1, WIN):
        perm = [(k, k // 8 * 8 + (k // 2 % 4 + dx) % 4 * 2 + k % 2) for k in range(32)]
        ring.append(lax.ppermute(mine, "expert", perm))
    own_t = jnp.stack(ring)
    oth_t = lax.ppermute(own_t, "expert", swap)

    near = [[8 * a + b for b in range(8)] for a in range(4)]
    tangents = lax.all_to_all(
        tangent, "dp", split_axis=0, concat_axis=0, tiled=True, axis_index_groups=near
    )

    def outer(flips, dtype):
        return call(
            functools.partial(outer_kernel, flips),
            sds((len(flips), hid, feats), dtype),
            [SMEM] + [VMEM] * 3,
            2 * len(flips) * hid * 1024 * CAP,
            2 << 20,
        )(at[:3], tangents, own_t, oth_t)

    def exchange(value, flip):
        perm = [
            (i * 32 + k, (flipped(i // ZLO, flip, k % 2) * ZLO + i % ZLO) * 32 + k)
            for i in range(ZN)
            for k in range(32)
        ]
        return lax.ppermute(value, DPX, perm)

    got = exchange(outer((1, 3), BF16), 1).astype(F32)
    here, there = outer((0, 2), F32)
    last = exchange((there + got[1]).astype(BF16), 2).astype(F32)
    return (here + got[0] + last).astype(BF16)


def solution(mesh):
    return jax.shard_map(
        on_device,
        mesh=mesh,
        in_specs=(
            P("dp", "expert"),
            P("dp", "expert"),
            P("dp", None),
            P("dp", None),
            P("expert", None),
            P("expert", None),
            P("expert", None),
            P("expert", None),
        ),
        out_specs=P("expert", "dp"),
        check_vma=False,
    )
```

```python
import functools

import jax
import jax.numpy as jnp
from jax import lax
from jax.experimental import pallas as pl
from jax.experimental.pallas import tpu as pltpu
from jax.sharding import PartitionSpec as P

WIN = 4
CAP = 128
ZN, ZLO, ZHI = 32, 8, 4
F32, BF16 = jnp.float32, jnp.bfloat16
DPX = ("dp", "expert")
SMEM = pl.BlockSpec(memory_space=pltpu.SMEM)
VMEM = pl.BlockSpec(memory_space=pltpu.VMEM)
HBM = pl.BlockSpec(memory_space=pltpu.HBM)
DMA = pltpu.SemaphoreType.DMA


def dot(a, b):
    return jnp.dot(a, b, preferred_element_type=F32)


def prep_kernel(ids_hbm, gates_hbm, tok_hbm, cot_hbm, send_ref, ids_ref, gates_ref, both_ref, sems):
    feats = tok_hbm.shape[1]
    copies = [
        pltpu.make_async_copy(ids_hbm, ids_ref, sems.at[0]),
        pltpu.make_async_copy(gates_hbm, gates_ref, sems.at[1]),
        pltpu.make_async_copy(tok_hbm, both_ref.at[:, pl.ds(0, feats)], sems.at[2]),
        pltpu.make_async_copy(cot_hbm, both_ref.at[:, pl.ds(feats, feats)], sems.at[3]),
    ]
    for copy in copies:
        copy.start()
    rows = tok_hbm.shape[0]
    upper = (
        lax.broadcasted_iota(jnp.int32, (CAP, CAP), 0)
        <= lax.broadcasted_iota(jnp.int32, (CAP, CAP), 1)
    ).astype(BF16)
    copies[0].wait()
    copies[1].wait()
    ids = ids_ref[...]
    gates = gates_ref[...]
    present, gate = [], []
    for j in range(WIN):
        named = ids == j
        present.append(jnp.max(jnp.where(named, 1.0, 0.0), axis=0, keepdims=True))
        gate.append(jnp.sum(jnp.where(named, gates, 0.0), axis=0, keepdims=True))
    marks = jnp.concatenate(present + present, axis=0)
    base = jnp.full((2 * WIN, 1), -1.0, F32)
    slots = []
    for b in range(rows // CAP):
        part = dot(marks[:, b * CAP : (b + 1) * CAP].astype(BF16), upper)
        slots.append(part + base)
        base = base + part[:, CAP - 1 :]
    slot = jnp.concatenate(slots, axis=1)
    slot = jnp.where(marks > 0.0, slot, -1.0).astype(jnp.int32)
    index = lax.broadcasted_iota(jnp.int32, (CAP, rows), 0)
    copies[2].wait()
    copies[3].wait()
    both = both_ref[...]
    for j in range(WIN):
        placer = slot[j : j + 1, :] == index
        got = dot(jnp.where(placer, 1.0, 0.0).astype(BF16), both)
        factor = jnp.sum(jnp.where(placer, gate[j], 0.0), axis=1, keepdims=True)
        xs = got[:, :feats]
        cs = got[:, feats:] * factor
        chunk = jnp.concatenate([xs.T, cs.T], axis=0).astype(BF16)
        for x in range(WIN):
            send_ref[j * WIN + x] = chunk


def pick_kernel(at_ref, rows_ref, out_ref):
    for y in range(WIN):
        out_ref[y] = rows_ref[y * WIN + at_ref[0], : out_ref.shape[1]]


def load(side, w_hbms, w_ref, sem):
    for n, w_hbm in enumerate(w_hbms):
        for s in range(w_hbm.shape[1] // (2 * CAP)):
            cols = pl.ds(pl.multiple_of((2 * s + side) * CAP, CAP), CAP)
            dst = w_ref.at[n, :, pl.ds(s * CAP, CAP)]
            pltpu.make_async_copy(w_hbm.at[:, cols], dst, sem.at[n]).start()


def half(rows_ref, w_ref, sem):
    chips, both, slots = rows_ref.shape
    xs = rows_ref[:, : both // 2].reshape(chips * both // 2, slots)
    cs = rows_ref[:, both // 2 :].reshape(chips * both // 2, slots)
    parts = []
    for n, rows in enumerate((xs, xs, xs, cs)):
        pltpu.make_async_copy(w_ref.at[n], w_ref.at[n], sem.at[n]).wait()
        parts.append(dot(w_ref[n], rows))
    return parts


def own_kernel(c_ref, rows_ref, g_hbm, u_hbm, p_hbm, d_hbm, acc_ref, w_ref, sem):
    load(c_ref[0], (g_hbm, u_hbm, p_hbm, d_hbm), w_ref, sem)
    for n, part in enumerate(half(rows_ref, w_ref, sem)):
        acc_ref[n] = part


def tangent_kernel(c_ref, rows_ref, g_hbm, u_hbm, p_hbm, d_hbm, acc_ref, out_ref, w_ref, sem):
    load(1 - c_ref[0], (g_hbm, u_hbm, p_hbm, d_hbm), w_ref, sem)
    preact, linear, probe_pre, backward = [
        acc_ref[n] + part for n, part in enumerate(half(rows_ref, w_ref, sem))
    ]
    sig = 1.0 / (1.0 + jnp.exp(-preact))
    curvature = sig * (1.0 - sig) * (2.0 + preact * (1.0 - 2.0 * sig))
    out_ref[...] = (backward * linear * curvature * probe_pre).astype(BF16)


def fan_kernel(tan_ref, moved_ref, out_ref, mine_ref):
    for i in range(ZLO):
        out_ref[i] = tan_ref[...]
    mine_ref[...] = moved_ref[...]


def outer_kernel(flips, at_ref, tan_ref, own_ref, oth_ref, out_ref):
    x, c, zhi = at_ref[0], at_ref[1], at_ref[2]
    for n, flip in enumerate(flips):
        dest = flipped(zhi, flip, c)
        acc = None
        for dx in range(WIN):
            chip = (x - dx + WIN) % WIN
            lhs = jnp.concatenate(
                [tan_ref[2 * chip + c], tan_ref[2 * chip + 1 - c]], axis=1
            )
            rhs = jnp.concatenate([own_ref[dx, dest], oth_ref[dx, dest]], axis=1)
            part = lax.dot_general(
                lhs, rhs, (((1,), (1,)), ((), ())), preferred_element_type=F32
            )
            acc = part if acc is None else acc + part
        out_ref[n] = acc.astype(out_ref.dtype)


def flipped(zhi, flip, core):
    near, mirror = zhi + 1 - 2 * (zhi % 2), 3 - zhi
    first = near + core * (mirror - near)
    return (zhi, first, near + mirror - first, (zhi + 2) % ZHI)[flip]


def call(kernel, out_shape, specs, flops, nbytes, scratch=(), **more):
    return pl.pallas_call(
        kernel,
        out_shape=out_shape,
        in_specs=specs,
        scratch_shapes=scratch,
        compiler_params=pltpu.CompilerParams(vmem_limit_bytes=16 << 20),
        cost_estimate=pl.CostEstimate(
            flops=flops, bytes_accessed=nbytes, transcendentals=0
        ),
        **({"out_specs": jax.tree.map(lambda _: VMEM, out_shape)} | more),
    )


def in_hbm(value):
    return pltpu.with_memory_space_constraint(value, pltpu.HBM)


def sds(shape, dtype):
    return jax.ShapeDtypeStruct(shape, dtype)


def on_device(tokens, cotangent, expert_ids, gate_values, gate_proj, up_proj, down_proj, probe):
    z, h = lax.axis_index("dp"), lax.axis_index("expert")
    x, c = (h // 2) % WIN, h % 2
    hid, feats = gate_proj.shape[0], tokens.shape[1]
    at = jnp.stack([x, c, z // ZLO, (x + z % ZLO // 2 + z % 2 + 2 * c) % WIN]).astype(jnp.int32)
    rows, cols = tokens.shape[0], gate_proj.shape[1]

    send = call(
        prep_kernel,
        sds((16, 2 * feats, CAP), BF16),
        [HBM] * 4,
        2 * 512 * 1024 * 256,
        2 << 20,
        [
            pltpu.VMEM((8, rows), jnp.int32),
            pltpu.VMEM((8, rows), F32),
            pltpu.VMEM((rows, 2 * feats), BF16),
            DMA((4,)),
        ],
    )(*map(in_hbm, (expert_ids.T, gate_values.T, tokens, cotangent)))

    same_core = [[c0 + 2 * i for i in range(16)] for c0 in range(2)]
    own = lax.all_to_all(
        send, "expert", split_axis=0, concat_axis=0, tiled=True, axis_index_groups=same_core
    )
    swap = [(i, i ^ 1) for i in range(32)]
    oth = lax.ppermute(own, "expert", swap)

    picked = call(
        pick_kernel, sds((WIN, feats, CAP), BF16), [SMEM, VMEM], 0, 1 << 18
    )(at[3:], own)
    perm = [
        (
            i * 32 + k,
            (i // 8 * 8 + (k // 2 + i % 8 // 2 + i % 2 + 2 * (k % 2)) % 4 * 2 + k % 2) * 32 + k // 8 * 8 + i % 8,
        )
        for i in range(ZN)
        for k in range(32)
    ]
    moved = lax.ppermute(picked, DPX, perm)

    weights = [in_hbm(w) for w in (gate_proj, up_proj, probe, down_proj)]
    columns = [pltpu.VMEM((4, hid, cols // 2), BF16), DMA((4,))]
    sums = call(
        own_kernel,
        sds((4, hid, CAP), F32),
        [SMEM, VMEM] + [HBM] * 4,
        4 * hid * cols * CAP,
        4 << 20,
        columns,
    )(at[1:2], own, *weights)
    tangent = call(
        tangent_kernel,
        sds((hid, CAP), BF16),
        [SMEM, VMEM] + [HBM] * 4 + [VMEM],
        4 * hid * cols * CAP,
        4 << 20,
        columns,
    )(at[1:2], oth, *weights, sums)

    tangent, mine = call(
        fan_kernel,
        [sds((ZLO, hid, CAP), BF16), sds((WIN, feats, CAP), BF16)],
        [VMEM, VMEM],
        0,
        1 << 19,
    )(tangent, moved)

    ring = [mine]
    for dx in range(1, WIN):
        perm = [(k, k // 8 * 8 + (k // 2 % 4 + dx) % 4 * 2 + k % 2) for k in range(32)]
        ring.append(lax.ppermute(mine, "expert", perm))
    own_t = jnp.stack(ring)
    oth_t = lax.ppermute(own_t, "expert", swap)

    near = [[8 * a + b for b in range(8)] for a in range(4)]
    tangents = lax.all_to_all(
        tangent, "dp", split_axis=0, concat_axis=0, tiled=True, axis_index_groups=near
    )

    def outer(flips, dtype):
        return call(
            functools.partial(outer_kernel, flips),
            sds((len(flips), hid, feats), dtype),
            [SMEM] + [VMEM] * 3,
            2 * len(flips) * hid * 1024 * CAP,
            2 << 20,
        )(at[:3], tangents, own_t, oth_t)

    def exchange(value, flip):
        perm = [
            (i * 32 + k, (flipped(i // ZLO, flip, k % 2) * ZLO + i % ZLO) * 32 + k)
            for i in range(ZN)
            for k in range(32)
        ]
        return lax.ppermute(value, DPX, perm)

    passed = exchange(outer((3,), BF16), 1)
    given = exchange(outer((1,), BF16), 1)
    mine = outer((0, 2), F32)
    last = exchange((mine[1:] + passed.astype(F32)).astype(BF16), 2)
    total = mine[:1] + given.astype(F32) + last.astype(F32)
    return total.astype(BF16)[0]


def solution(mesh):
    return jax.shard_map(
        on_device,
        mesh=mesh,
        in_specs=(
            P("dp", "expert"),
            P("dp", "expert"),
            P("dp", None),
            P("dp", None),
            P("expert", None),
            P("expert", None),
            P("expert", None),
            P("expert", None),
        ),
        out_specs=P("expert", "dp"),
        check_vma=False,
    )
```

```python
import functools

import jax
import jax.numpy as jnp
from jax import lax
from jax.experimental import pallas as pl
from jax.experimental.pallas import tpu as pltpu
from jax.sharding import PartitionSpec as P

WIN = 4
CAP = 128
ZN, ZLO, ZHI = 32, 8, 4
F32, BF16 = jnp.float32, jnp.bfloat16
DPX = ("dp", "expert")
SMEM = pl.BlockSpec(memory_space=pltpu.SMEM)
VMEM = pl.BlockSpec(memory_space=pltpu.VMEM)
HBM = pl.BlockSpec(memory_space=pltpu.HBM)
DMA = pltpu.SemaphoreType.DMA


def dot(a, b):
    return jnp.dot(a, b, preferred_element_type=F32)


def prep_kernel(ids_hbm, gates_hbm, tok_hbm, cot_hbm, send_ref, ids_ref, gates_ref, both_ref, sems):
    feats = tok_hbm.shape[1]
    copies = [
        pltpu.make_async_copy(ids_hbm, ids_ref, sems.at[0]),
        pltpu.make_async_copy(gates_hbm, gates_ref, sems.at[1]),
        pltpu.make_async_copy(tok_hbm, both_ref.at[:, pl.ds(0, feats)], sems.at[2]),
        pltpu.make_async_copy(cot_hbm, both_ref.at[:, pl.ds(feats, feats)], sems.at[3]),
    ]
    for copy in copies:
        copy.start()
    rows = tok_hbm.shape[0]
    upper = (
        lax.broadcasted_iota(jnp.int32, (CAP, CAP), 0)
        <= lax.broadcasted_iota(jnp.int32, (CAP, CAP), 1)
    ).astype(BF16)
    copies[0].wait()
    copies[1].wait()
    ids = ids_ref[...]
    gates = gates_ref[...]
    present, gate = [], []
    for j in range(WIN):
        named = ids == j
        present.append(jnp.max(jnp.where(named, 1.0, 0.0), axis=0, keepdims=True))
        gate.append(jnp.sum(jnp.where(named, gates, 0.0), axis=0, keepdims=True))
    marks = jnp.concatenate(present + present, axis=0)
    base = jnp.full((2 * WIN, 1), -1.0, F32)
    slots = []
    for b in range(rows // CAP):
        part = dot(marks[:, b * CAP : (b + 1) * CAP].astype(BF16), upper)
        slots.append(part + base)
        base = base + part[:, CAP - 1 :]
    slot = jnp.concatenate(slots, axis=1)
    slot = jnp.where(marks > 0.0, slot, -1.0).astype(jnp.int32)
    index = lax.broadcasted_iota(jnp.int32, (CAP, rows), 0)
    copies[2].wait()
    copies[3].wait()
    both = both_ref[...]
    for j in range(WIN):
        placer = slot[j : j + 1, :] == index
        got = dot(jnp.where(placer, 1.0, 0.0).astype(BF16), both)
        factor = jnp.sum(jnp.where(placer, gate[j], 0.0), axis=1, keepdims=True)
        xs = got[:, :feats]
        cs = got[:, feats:] * factor
        chunk = jnp.concatenate([xs.T, cs.T], axis=0).astype(BF16)
        for x in range(WIN):
            send_ref[j * WIN + x] = chunk


def pick_kernel(at_ref, rows_ref, out_ref):
    for y in range(WIN):
        out_ref[y] = rows_ref[y * WIN + at_ref[0], : out_ref.shape[1]]


def load(side, w_hbms, w_ref, sem):
    for n, w_hbm in enumerate(w_hbms):
        for s in range(w_hbm.shape[1] // (2 * CAP)):
            cols = pl.ds(pl.multiple_of((2 * s + side) * CAP, CAP), CAP)
            dst = w_ref.at[n, :, pl.ds(s * CAP, CAP)]
            pltpu.make_async_copy(w_hbm.at[:, cols], dst, sem.at[n]).start()


def half(rows_ref, w_ref, sem):
    chips, both, slots = rows_ref.shape
    xs = rows_ref[:, : both // 2].reshape(chips * both // 2, slots)
    cs = rows_ref[:, both // 2 :].reshape(chips * both // 2, slots)
    parts = []
    for n, rows in enumerate((xs, xs, xs, cs)):
        pltpu.make_async_copy(w_ref.at[n], w_ref.at[n], sem.at[n]).wait()
        parts.append(dot(w_ref[n], rows))
    return parts


def own_kernel(c_ref, rows_ref, g_hbm, u_hbm, p_hbm, d_hbm, acc_ref, w_ref, sem):
    load(c_ref[0], (g_hbm, u_hbm, p_hbm, d_hbm), w_ref, sem)
    for n, part in enumerate(half(rows_ref, w_ref, sem)):
        acc_ref[n] = part


def tangent_kernel(c_ref, rows_ref, g_hbm, u_hbm, p_hbm, d_hbm, acc_ref, out_ref, w_ref, sem):
    load(1 - c_ref[0], (g_hbm, u_hbm, p_hbm, d_hbm), w_ref, sem)
    preact, linear, probe_pre, backward = [
        acc_ref[n] + part for n, part in enumerate(half(rows_ref, w_ref, sem))
    ]
    sig = 1.0 / (1.0 + jnp.exp(-preact))
    curvature = sig * (1.0 - sig) * (2.0 + preact * (1.0 - 2.0 * sig))
    out_ref[...] = (backward * linear * curvature * probe_pre).astype(BF16)


def fan_kernel(tan_ref, moved_ref, out_ref, mine_ref):
    for i in range(ZLO):
        out_ref[i] = tan_ref[...]
    mine_ref[...] = moved_ref[...]


def outer_kernel(flips, at_ref, tan_ref, own_ref, oth_ref, out_ref):
    x, c, zhi, turn = at_ref[0], at_ref[1], at_ref[2], at_ref[3]
    for n, flip in enumerate(flips):
        dest = flipped(zhi, flip, c)
        acc = None
        for dx in range(WIN):
            chip = (x - dx + WIN) % WIN
            blocks = [(turn - chip - core) % WIN * 2 + core for core in (c, 1 - c)]
            lhs = jnp.concatenate([tan_ref[b] for b in blocks], axis=1)
            rhs = jnp.concatenate([own_ref[dx, dest], oth_ref[dx, dest]], axis=1)
            part = lax.dot_general(
                lhs, rhs, (((1,), (1,)), ((), ())), preferred_element_type=F32
            )
            acc = part if acc is None else acc + part
        out_ref[n] = acc.astype(out_ref.dtype)


def flipped(zhi, flip, core):
    near, mirror = zhi + 1 - 2 * (zhi % 2), 3 - zhi
    first = near + core * (mirror - near)
    return (zhi, first, near + mirror - first, (zhi + 2) % ZHI)[flip]


def call(kernel, out_shape, specs, flops, nbytes, scratch=(), **more):
    return pl.pallas_call(
        kernel,
        out_shape=out_shape,
        in_specs=specs,
        scratch_shapes=scratch,
        compiler_params=pltpu.CompilerParams(vmem_limit_bytes=16 << 20),
        cost_estimate=pl.CostEstimate(
            flops=flops, bytes_accessed=nbytes, transcendentals=0
        ),
        **({"out_specs": jax.tree.map(lambda _: VMEM, out_shape)} | more),
    )


def in_hbm(value):
    return pltpu.with_memory_space_constraint(value, pltpu.HBM)


def sds(shape, dtype):
    return jax.ShapeDtypeStruct(shape, dtype)


def on_device(tokens, cotangent, expert_ids, gate_values, gate_proj, up_proj, down_proj, probe):
    z, h = lax.axis_index("dp"), lax.axis_index("expert")
    x, c = (h // 2) % WIN, h % 2
    hid, feats = gate_proj.shape[0], tokens.shape[1]
    low = z % ZLO
    turn = low // 2 - 2 * (low % 2) + 2 * WIN
    pick = (x + low // 2 + low % 2 + 2 * c) % WIN
    at = jnp.stack([x, c, z // ZLO, turn, pick]).astype(jnp.int32)
    rows, cols = tokens.shape[0], gate_proj.shape[1]

    send = call(
        prep_kernel,
        sds((16, 2 * feats, CAP), BF16),
        [HBM] * 4,
        2 * 512 * 1024 * 256,
        2 << 20,
        [
            pltpu.VMEM((8, rows), jnp.int32),
            pltpu.VMEM((8, rows), F32),
            pltpu.VMEM((rows, 2 * feats), BF16),
            DMA((4,)),
        ],
    )(*map(in_hbm, (expert_ids.T, gate_values.T, tokens, cotangent)))

    same_core = [[c0 + 2 * i for i in range(16)] for c0 in range(2)]
    own = lax.all_to_all(
        send, "expert", split_axis=0, concat_axis=0, tiled=True, axis_index_groups=same_core
    )
    swap = [(i, i ^ 1) for i in range(32)]
    oth = lax.ppermute(own, "expert", swap)

    picked = call(
        pick_kernel, sds((WIN, feats, CAP), BF16), [SMEM, VMEM], 0, 1 << 18
    )(at[4:], own)
    perm = [
        (
            i * 32 + k,
            (i // 8 * 8 + (k // 2 + i % 8 // 2 + i % 2 + 2 * (k % 2)) % 4 * 2 + k % 2) * 32
            + k // 2 * 2
            + i % 2,
        )
        for i in range(ZN)
        for k in range(32)
    ]
    moved = lax.ppermute(picked, DPX, perm)

    weights = [in_hbm(w) for w in (gate_proj, up_proj, probe, down_proj)]
    columns = [pltpu.VMEM((4, hid, cols // 2), BF16), DMA((4,))]
    sums = call(
        own_kernel,
        sds((4, hid, CAP), F32),
        [SMEM, VMEM] + [HBM] * 4,
        4 * hid * cols * CAP,
        4 << 20,
        columns,
    )(at[1:2], own, *weights)
    tangent = call(
        tangent_kernel,
        sds((hid, CAP), BF16),
        [SMEM, VMEM] + [HBM] * 4 + [VMEM],
        4 * hid * cols * CAP,
        4 << 20,
        columns,
    )(at[1:2], oth, *weights, sums)

    tangent, mine = call(
        fan_kernel,
        [sds((ZLO, hid, CAP), BF16), sds((WIN, feats, CAP), BF16)],
        [VMEM, VMEM],
        0,
        1 << 19,
    )(tangent, moved)

    ring = [mine]
    for dx in range(1, WIN):
        perm = [(k, k // 8 * 8 + (k // 2 % 4 + dx) % 4 * 2 + k % 2) for k in range(32)]
        ring.append(lax.ppermute(mine, "expert", perm))
    own_t = jnp.stack(ring)
    oth_t = lax.ppermute(own_t, "expert", swap)

    near = [[8 * a + b for b in range(8)] for a in range(4)]
    tangents = lax.all_to_all(
        tangent, "dp", split_axis=0, concat_axis=0, tiled=True, axis_index_groups=near
    )

    def outer(flips, dtype):
        return call(
            functools.partial(outer_kernel, flips),
            sds((len(flips), hid, feats), dtype),
            [SMEM] + [VMEM] * 3,
            2 * len(flips) * hid * 1024 * CAP,
            2 << 20,
        )(at[:4], tangents, own_t, oth_t)

    def exchange(value, flip):
        perm = [
            (i * 32 + k, (flipped(i // ZLO, flip, k % 2) * ZLO + i % ZLO) * 32 + k)
            for i in range(ZN)
            for k in range(32)
        ]
        return lax.ppermute(value, DPX, perm)

    passed = exchange(outer((3,), BF16), 1)
    given = exchange(outer((1,), BF16), 1)
    mine = outer((0, 2), F32)
    last = exchange((mine[1:] + passed.astype(F32)).astype(BF16), 2)
    total = mine[:1] + given.astype(F32) + last.astype(F32)
    return total.astype(BF16)[0]


def solution(mesh):
    return jax.shard_map(
        on_device,
        mesh=mesh,
        in_specs=(
            P("dp", "expert"),
            P("dp", "expert"),
            P("dp", None),
            P("dp", None),
            P("expert", None),
            P("expert", None),
            P("expert", None),
            P("expert", None),
        ),
        out_specs=P("expert", "dp"),
        check_vma=False,
    )
```

```python
import functools

import jax
import jax.numpy as jnp
from jax import lax
from jax.experimental import pallas as pl
from jax.experimental.pallas import tpu as pltpu
from jax.sharding import PartitionSpec as P

WIN = 4
CAP = 128
ZN, ZLO, ZHI = 32, 8, 4
F32, BF16 = jnp.float32, jnp.bfloat16
DPX = ("dp", "expert")
SMEM = pl.BlockSpec(memory_space=pltpu.SMEM)
VMEM = pl.BlockSpec(memory_space=pltpu.VMEM)
ANY = pl.BlockSpec(memory_space=pl.ANY)
HBM = pl.BlockSpec(memory_space=pltpu.HBM)
DMA = pltpu.SemaphoreType.DMA


def dot(a, b):
    return jnp.dot(a, b, preferred_element_type=F32)


def prep_kernel(ids_hbm, gates_hbm, tok_hbm, cot_hbm, send_ref, ids_ref, gates_ref, both_ref, sems):
    feats = tok_hbm.shape[1]
    copies = [
        pltpu.make_async_copy(ids_hbm, ids_ref, sems.at[0]),
        pltpu.make_async_copy(gates_hbm, gates_ref, sems.at[1]),
        pltpu.make_async_copy(tok_hbm, both_ref.at[:, pl.ds(0, feats)], sems.at[2]),
        pltpu.make_async_copy(cot_hbm, both_ref.at[:, pl.ds(feats, feats)], sems.at[3]),
    ]
    for copy in copies:
        copy.start()
    rows = tok_hbm.shape[0]
    upper = (
        lax.broadcasted_iota(jnp.int32, (CAP, CAP), 0)
        <= lax.broadcasted_iota(jnp.int32, (CAP, CAP), 1)
    ).astype(BF16)
    copies[0].wait()
    copies[1].wait()
    ids = ids_ref[...]
    gates = gates_ref[...]
    present, gate = [], []
    for j in range(WIN):
        named = ids == j
        present.append(jnp.max(jnp.where(named, 1.0, 0.0), axis=0, keepdims=True))
        gate.append(jnp.sum(jnp.where(named, gates, 0.0), axis=0, keepdims=True))
    marks = jnp.concatenate(present + present, axis=0)
    base = jnp.full((2 * WIN, 1), -1.0, F32)
    slots = []
    for b in range(rows // CAP):
        part = dot(marks[:, b * CAP : (b + 1) * CAP].astype(BF16), upper)
        slots.append(part + base)
        base = base + part[:, CAP - 1 :]
    slot = jnp.concatenate(slots, axis=1)
    slot = jnp.where(marks > 0.0, slot, -1.0).astype(jnp.int32)
    index = lax.broadcasted_iota(jnp.int32, (CAP, rows), 0)
    copies[2].wait()
    copies[3].wait()
    both = both_ref[...]
    for j in range(WIN):
        placer = slot[j : j + 1, :] == index
        got = dot(jnp.where(placer, 1.0, 0.0).astype(BF16), both)
        factor = jnp.sum(jnp.where(placer, gate[j], 0.0), axis=1, keepdims=True)
        xs = got[:, :feats]
        cs = got[:, feats:] * factor
        chunk = jnp.concatenate([xs.T, cs.T], axis=0).astype(BF16)
        for x in range(WIN):
            send_ref[j * WIN + x] = chunk


def pick_kernel(at_ref, rows_ref, out_ref):
    for y in range(WIN):
        out_ref[y] = rows_ref[y * WIN + at_ref[0], : out_ref.shape[1]]


def load(side, w_hbms, w_ref, sem):
    for n, w_hbm in enumerate(w_hbms):
        for s in range(w_hbm.shape[1] // (2 * CAP)):
            cols = pl.ds(pl.multiple_of((2 * s + side) * CAP, CAP), CAP)
            dst = w_ref.at[n, :, pl.ds(s * CAP, CAP)]
            pltpu.make_async_copy(w_hbm.at[:, cols], dst, sem.at[n]).start()


def half(rows_ref, w_ref, sem):
    chips, both, slots = rows_ref.shape
    xs = rows_ref[:, : both // 2].reshape(chips * both // 2, slots)
    cs = rows_ref[:, both // 2 :].reshape(chips * both // 2, slots)
    parts = []
    for n, rows in enumerate((xs, xs, xs, cs)):
        pltpu.make_async_copy(w_ref.at[n], w_ref.at[n], sem.at[n]).wait()
        parts.append(dot(w_ref[n], rows))
    return parts


def own_kernel(c_ref, rows_ref, g_hbm, u_hbm, p_hbm, d_hbm, acc_ref, w_ref, sem):
    load(c_ref[0], (g_hbm, u_hbm, p_hbm, d_hbm), w_ref, sem)
    for n, part in enumerate(half(rows_ref, w_ref, sem)):
        acc_ref[n] = part


def tangent_kernel(c_ref, rows_ref, g_hbm, u_hbm, p_hbm, d_hbm, acc_ref, out_ref, w_ref, sem):
    load(1 - c_ref[0], (g_hbm, u_hbm, p_hbm, d_hbm), w_ref, sem)
    preact, linear, probe_pre, backward = [
        acc_ref[n] + part for n, part in enumerate(half(rows_ref, w_ref, sem))
    ]
    sig = 1.0 / (1.0 + jnp.exp(-preact))
    curvature = sig * (1.0 - sig) * (2.0 + preact * (1.0 - 2.0 * sig))
    out_ref[...] = (backward * linear * curvature * probe_pre).astype(BF16)


def fan_kernel(tan_ref, moved_ref, out_ref, mine_ref, sems):
    del moved_ref, mine_ref
    copies = [
        pltpu.make_async_copy(tan_ref, out_ref.at[i], sems.at[i]) for i in range(ZLO)
    ]
    for copy in copies:
        copy.start()
    for copy in copies:
        copy.wait()


def outer_kernel(flips, at_ref, tan_ref, own_ref, oth_ref, out_ref):
    x, c, zhi, turn = at_ref[0], at_ref[1], at_ref[2], at_ref[3]
    for n, flip in enumerate(flips):
        dest = flipped(zhi, flip, c)
        acc = None
        for dx in range(WIN):
            chip = (x - dx + WIN) % WIN
            blocks = [(turn - chip - core) % WIN * 2 + core for core in (c, 1 - c)]
            lhs = jnp.concatenate([tan_ref[b] for b in blocks], axis=1)
            rhs = jnp.concatenate([own_ref[dx, dest], oth_ref[dx, dest]], axis=1)
            part = lax.dot_general(
                lhs, rhs, (((1,), (1,)), ((), ())), preferred_element_type=F32
            )
            acc = part if acc is None else acc + part
        out_ref[n] = acc.astype(out_ref.dtype)


def flipped(zhi, flip, core):
    near, mirror = zhi + 1 - 2 * (zhi % 2), 3 - zhi
    first = near + core * (mirror - near)
    return (zhi, first, near + mirror - first, (zhi + 2) % ZHI)[flip]


def call(kernel, out_shape, specs, flops, nbytes, scratch=(), **more):
    return pl.pallas_call(
        kernel,
        out_shape=out_shape,
        in_specs=specs,
        scratch_shapes=scratch,
        compiler_params=pltpu.CompilerParams(vmem_limit_bytes=16 << 20),
        cost_estimate=pl.CostEstimate(
            flops=flops, bytes_accessed=nbytes, transcendentals=0
        ),
        **({"out_specs": jax.tree.map(lambda _: VMEM, out_shape)} | more),
    )


def in_hbm(value):
    return pltpu.with_memory_space_constraint(value, pltpu.HBM)


def sds(shape, dtype):
    return jax.ShapeDtypeStruct(shape, dtype)


def on_device(tokens, cotangent, expert_ids, gate_values, gate_proj, up_proj, down_proj, probe):
    z, h = lax.axis_index("dp"), lax.axis_index("expert")
    x, c = (h // 2) % WIN, h % 2
    hid, feats = gate_proj.shape[0], tokens.shape[1]
    low = z % ZLO
    turn = low // 2 - 2 * (low % 2) + 2 * WIN
    pick = (x + low // 2 + low % 2 + 2 * c) % WIN
    at = jnp.stack([x, c, z // ZLO, turn, pick]).astype(jnp.int32)
    rows, cols = tokens.shape[0], gate_proj.shape[1]

    send = call(
        prep_kernel,
        sds((16, 2 * feats, CAP), BF16),
        [HBM] * 4,
        2 * 512 * 1024 * 256,
        2 << 20,
        [
            pltpu.VMEM((8, rows), jnp.int32),
            pltpu.VMEM((8, rows), F32),
            pltpu.VMEM((rows, 2 * feats), BF16),
            DMA((4,)),
        ],
    )(*map(in_hbm, (expert_ids.T, gate_values.T, tokens, cotangent)))

    same_core = [[c0 + 2 * i for i in range(16)] for c0 in range(2)]
    own = lax.all_to_all(
        send, "expert", split_axis=0, concat_axis=0, tiled=True, axis_index_groups=same_core
    )
    swap = [(i, i ^ 1) for i in range(32)]
    oth = lax.ppermute(own, "expert", swap)

    picked = call(
        pick_kernel, sds((WIN, feats, CAP), BF16), [SMEM, VMEM], 0, 1 << 18
    )(at[4:], own)
    perm = [
        (
            i * 32 + k,
            (i // 8 * 8 + (k // 2 + i % 8 // 2 + i % 2 + 2 * (k % 2)) % 4 * 2 + k % 2) * 32
            + k // 2 * 2
            + i % 2,
        )
        for i in range(ZN)
        for k in range(32)
    ]
    moved = lax.ppermute(picked, DPX, perm)

    weights = [in_hbm(w) for w in (gate_proj, up_proj, probe, down_proj)]
    columns = [pltpu.VMEM((4, hid, cols // 2), BF16), DMA((4,))]
    sums = call(
        own_kernel,
        sds((4, hid, CAP), F32),
        [SMEM, VMEM] + [HBM] * 4,
        4 * hid * cols * CAP,
        4 << 20,
        columns,
    )(at[1:2], own, *weights)
    tangent = call(
        tangent_kernel,
        sds((hid, CAP), BF16),
        [SMEM, VMEM] + [HBM] * 4 + [VMEM],
        4 * hid * cols * CAP,
        4 << 20,
        columns,
    )(at[1:2], oth, *weights, sums)

    tangent, mine = call(
        fan_kernel,
        [sds((ZLO, hid, CAP), BF16), sds((WIN, feats, CAP), BF16)],
        [VMEM, ANY],
        0,
        1 << 19,
        [DMA((ZLO,))],
        out_specs=[ANY, ANY],
        input_output_aliases={1: 1},
    )(tangent, moved)

    ring = [mine]
    for dx in range(1, WIN):
        perm = [(k, k // 8 * 8 + (k // 2 % 4 + dx) % 4 * 2 + k % 2) for k in range(32)]
        ring.append(lax.ppermute(mine, "expert", perm))
    own_t = jnp.stack(ring)
    oth_t = lax.ppermute(own_t, "expert", swap)

    near = [[8 * a + b for b in range(8)] for a in range(4)]
    tangents = lax.all_to_all(
        tangent, "dp", split_axis=0, concat_axis=0, tiled=True, axis_index_groups=near
    )

    def outer(flips, dtype):
        return call(
            functools.partial(outer_kernel, flips),
            sds((len(flips), hid, feats), dtype),
            [SMEM] + [VMEM] * 3,
            2 * len(flips) * hid * 1024 * CAP,
            2 << 20,
        )(at[:4], tangents, own_t, oth_t)

    def exchange(value, flip):
        perm = [
            (i * 32 + k, (flipped(i // ZLO, flip, k % 2) * ZLO + i % ZLO) * 32 + k)
            for i in range(ZN)
            for k in range(32)
        ]
        return lax.ppermute(value, DPX, perm)

    passed = exchange(outer((3,), BF16), 1)
    given = exchange(outer((1,), BF16), 1)
    mine = outer((0, 2), F32)
    last = exchange((mine[1:] + passed.astype(F32)).astype(BF16), 2)
    total = mine[:1] + given.astype(F32) + last.astype(F32)
    return total.astype(BF16)[0]


def solution(mesh):
    return jax.shard_map(
        on_device,
        mesh=mesh,
        in_specs=(
            P("dp", "expert"),
            P("dp", "expert"),
            P("dp", None),
            P("dp", None),
            P("expert", None),
            P("expert", None),
            P("expert", None),
            P("expert", None),
        ),
        out_specs=P("expert", "dp"),
        check_vma=False,
    )
```

```python
import functools

import jax
import jax.numpy as jnp
from jax import lax
from jax.experimental import pallas as pl
from jax.experimental.pallas import tpu as pltpu
from jax.sharding import PartitionSpec as P

WIN = 4
CAP = 128
ZN, ZLO, ZHI = 32, 8, 4
F32, BF16 = jnp.float32, jnp.bfloat16
DPX = ("dp", "expert")
SMEM = pl.BlockSpec(memory_space=pltpu.SMEM)
VMEM = pl.BlockSpec(memory_space=pltpu.VMEM)
ANY = pl.BlockSpec(memory_space=pl.ANY)
HBM = pl.BlockSpec(memory_space=pltpu.HBM)
DMA = pltpu.SemaphoreType.DMA


def dot(a, b):
    return jnp.dot(a, b, preferred_element_type=F32)


def prep_kernel(ids_hbm, gates_hbm, tok_hbm, cot_hbm, send_ref, ids_ref, gates_ref, both_ref, sems):
    feats = tok_hbm.shape[1]
    copies = [
        pltpu.make_async_copy(ids_hbm, ids_ref, sems.at[0]),
        pltpu.make_async_copy(gates_hbm, gates_ref, sems.at[1]),
        pltpu.make_async_copy(tok_hbm, both_ref.at[:, pl.ds(0, feats)], sems.at[2]),
        pltpu.make_async_copy(cot_hbm, both_ref.at[:, pl.ds(feats, feats)], sems.at[3]),
    ]
    for copy in copies:
        copy.start()
    rows = tok_hbm.shape[0]
    upper = (
        lax.broadcasted_iota(jnp.int32, (CAP, CAP), 0)
        <= lax.broadcasted_iota(jnp.int32, (CAP, CAP), 1)
    ).astype(BF16)
    copies[0].wait()
    copies[1].wait()
    ids = ids_ref[...]
    gates = gates_ref[...]
    present, gate = [], []
    for j in range(WIN):
        named = ids == j
        present.append(jnp.max(jnp.where(named, 1.0, 0.0), axis=0, keepdims=True))
        gate.append(jnp.sum(jnp.where(named, gates, 0.0), axis=0, keepdims=True))
    marks = jnp.concatenate(present + present, axis=0)
    base = jnp.full((2 * WIN, 1), -1.0, F32)
    slots = []
    for b in range(rows // CAP):
        part = dot(marks[:, b * CAP : (b + 1) * CAP].astype(BF16), upper)
        slots.append(part + base)
        base = base + part[:, CAP - 1 :]
    slot = jnp.concatenate(slots, axis=1)
    slot = jnp.where(marks > 0.0, slot, -1.0).astype(jnp.int32)
    index = lax.broadcasted_iota(jnp.int32, (CAP, rows), 0)
    copies[2].wait()
    copies[3].wait()
    both = both_ref[...]
    for j in range(WIN):
        placer = slot[j : j + 1, :] == index
        got = dot(jnp.where(placer, 1.0, 0.0).astype(BF16), both)
        factor = jnp.sum(jnp.where(placer, gate[j], 0.0), axis=1, keepdims=True)
        xs = got[:, :feats]
        cs = got[:, feats:] * factor
        chunk = jnp.concatenate([xs.T, cs.T], axis=0).astype(BF16)
        for x in range(WIN):
            send_ref[j * WIN + x] = chunk


def pick_kernel(at_ref, rows_ref, out_ref):
    for y in range(WIN):
        out_ref[y] = rows_ref[y * WIN + at_ref[0], : out_ref.shape[1]]


def load(side, w_hbms, w_ref, sem):
    for n, w_hbm in enumerate(w_hbms):
        for s in range(w_hbm.shape[1] // (2 * CAP)):
            cols = pl.ds(pl.multiple_of((2 * s + side) * CAP, CAP), CAP)
            dst = w_ref.at[n, :, pl.ds(s * CAP, CAP)]
            pltpu.make_async_copy(w_hbm.at[:, cols], dst, sem.at[n]).start()


def half(rows_ref, w_ref, sem):
    chips, both, slots = rows_ref.shape
    xs = rows_ref[:, : both // 2].reshape(chips * both // 2, slots)
    cs = rows_ref[:, both // 2 :].reshape(chips * both // 2, slots)
    parts = []
    for n, rows in enumerate((xs, xs, xs, cs)):
        pltpu.make_async_copy(w_ref.at[n], w_ref.at[n], sem.at[n]).wait()
        parts.append(dot(w_ref[n], rows))
    return parts


def own_kernel(c_ref, rows_ref, g_hbm, u_hbm, p_hbm, d_hbm, acc_ref, w_ref, sem):
    load(c_ref[0], (g_hbm, u_hbm, p_hbm, d_hbm), w_ref, sem)
    for n, part in enumerate(half(rows_ref, w_ref, sem)):
        acc_ref[n] = part


def tangent_kernel(c_ref, rows_ref, g_hbm, u_hbm, p_hbm, d_hbm, acc_ref, out_ref, w_ref, sem):
    load(1 - c_ref[0], (g_hbm, u_hbm, p_hbm, d_hbm), w_ref, sem)
    preact, linear, probe_pre, backward = [
        acc_ref[n] + part for n, part in enumerate(half(rows_ref, w_ref, sem))
    ]
    sig = 1.0 / (1.0 + jnp.exp(-preact))
    curvature = sig * (1.0 - sig) * (2.0 + preact * (1.0 - 2.0 * sig))
    out_ref[...] = (backward * linear * curvature * probe_pre).astype(BF16)


def fan_kernel(tan_ref, moved_ref, out_ref, mine_ref, sems):
    del moved_ref, mine_ref
    copies = [
        pltpu.make_async_copy(tan_ref, out_ref.at[i], sems.at[i]) for i in range(ZLO)
    ]
    for copy in copies:
        copy.start()
    for copy in copies:
        copy.wait()


def outer_kernel(flips, at_ref, tan_ref, own_ref, oth_ref, out_ref):
    c, zhi, turn = at_ref[0], at_ref[1], at_ref[2]
    for n, flip in enumerate(flips):
        dest = flipped(zhi, flip, c)
        acc = None
        for chip in range(WIN):
            blocks = [(turn - chip - core) % WIN * 2 + core for core in (c, 1 - c)]
            lhs = jnp.concatenate([tan_ref[b] for b in blocks], axis=1)
            rhs = jnp.concatenate([own_ref[chip, dest], oth_ref[chip, dest]], axis=1)
            part = lax.dot_general(
                lhs, rhs, (((1,), (1,)), ((), ())), preferred_element_type=F32
            )
            acc = part if acc is None else acc + part
        out_ref[n] = acc.astype(out_ref.dtype)


def flipped(zhi, flip, core):
    near, mirror = zhi + 1 - 2 * (zhi % 2), 3 - zhi
    first = near + core * (mirror - near)
    return (zhi, first, near + mirror - first, (zhi + 2) % ZHI)[flip]


def call(kernel, out_shape, specs, flops, nbytes, scratch=(), **more):
    return pl.pallas_call(
        kernel,
        out_shape=out_shape,
        in_specs=specs,
        scratch_shapes=scratch,
        compiler_params=pltpu.CompilerParams(vmem_limit_bytes=16 << 20),
        cost_estimate=pl.CostEstimate(
            flops=flops, bytes_accessed=nbytes, transcendentals=0
        ),
        **({"out_specs": jax.tree.map(lambda _: VMEM, out_shape)} | more),
    )


def in_hbm(value):
    return pltpu.with_memory_space_constraint(value, pltpu.HBM)


def sds(shape, dtype):
    return jax.ShapeDtypeStruct(shape, dtype)


def on_device(tokens, cotangent, expert_ids, gate_values, gate_proj, up_proj, down_proj, probe):
    z, h = lax.axis_index("dp"), lax.axis_index("expert")
    x, c = (h // 2) % WIN, h % 2
    hid, feats = gate_proj.shape[0], tokens.shape[1]
    low = z % ZLO
    turn = low // 2 - 2 * (low % 2) + 2 * WIN
    pick = (x + low // 2 + low % 2 + 2 * c) % WIN
    at = jnp.stack([x, c, z // ZLO, turn, pick]).astype(jnp.int32)
    rows, cols = tokens.shape[0], gate_proj.shape[1]

    send = call(
        prep_kernel,
        sds((16, 2 * feats, CAP), BF16),
        [HBM] * 4,
        2 * 512 * 1024 * 256,
        2 << 20,
        [
            pltpu.VMEM((8, rows), jnp.int32),
            pltpu.VMEM((8, rows), F32),
            pltpu.VMEM((rows, 2 * feats), BF16),
            DMA((4,)),
        ],
    )(*map(in_hbm, (expert_ids.T, gate_values.T, tokens, cotangent)))

    same_core = [[c0 + 2 * i for i in range(16)] for c0 in range(2)]
    own = lax.all_to_all(
        send, "expert", split_axis=0, concat_axis=0, tiled=True, axis_index_groups=same_core
    )
    swap = [(i, i ^ 1) for i in range(32)]
    oth = lax.ppermute(own, "expert", swap)

    picked = call(
        pick_kernel, sds((WIN, feats, CAP), BF16), [SMEM, VMEM], 0, 1 << 18
    )(at[4:], own)
    perm = [
        (
            i * 32 + k,
            (i // 8 * 8 + (k // 2 + i % 8 // 2 + i % 2 + 2 * (k % 2)) % 4 * 2 + k % 2) * 32
            + k // 2 * 2
            + i % 2,
        )
        for i in range(ZN)
        for k in range(32)
    ]
    moved = lax.ppermute(picked, DPX, perm)

    weights = [in_hbm(w) for w in (gate_proj, up_proj, probe, down_proj)]
    columns = [pltpu.VMEM((4, hid, cols // 2), BF16), DMA((4,))]
    sums = call(
        own_kernel,
        sds((4, hid, CAP), F32),
        [SMEM, VMEM] + [HBM] * 4,
        4 * hid * cols * CAP,
        4 << 20,
        columns,
    )(at[1:2], own, *weights)
    tangent = call(
        tangent_kernel,
        sds((hid, CAP), BF16),
        [SMEM, VMEM] + [HBM] * 4 + [VMEM],
        4 * hid * cols * CAP,
        4 << 20,
        columns,
    )(at[1:2], oth, *weights, sums)

    tangent, mine = call(
        fan_kernel,
        [sds((ZLO, hid, CAP), BF16), sds((WIN, feats, CAP), BF16)],
        [VMEM, ANY],
        0,
        1 << 19,
        [DMA((ZLO,))],
        out_specs=[ANY, ANY],
        input_output_aliases={1: 1},
    )(tangent, moved)

    row = [[8 * y + c0 + 2 * i for i in range(WIN)] for y in range(WIN) for c0 in range(2)]
    own_t = lax.all_gather(mine, "expert", axis_index_groups=row)
    oth_t = lax.ppermute(own_t, "expert", swap)

    near = [[8 * a + b for b in range(8)] for a in range(4)]
    tangents = lax.all_to_all(
        tangent, "dp", split_axis=0, concat_axis=0, tiled=True, axis_index_groups=near
    )

    def outer(flips, dtype):
        return call(
            functools.partial(outer_kernel, flips),
            sds((len(flips), hid, feats), dtype),
            [SMEM] + [VMEM] * 3,
            2 * len(flips) * hid * 1024 * CAP,
            2 << 20,
        )(at[1:4], tangents, own_t, oth_t)

    def exchange(value, flip):
        perm = [
            (i * 32 + k, (flipped(i // ZLO, flip, k % 2) * ZLO + i % ZLO) * 32 + k)
            for i in range(ZN)
            for k in range(32)
        ]
        return lax.ppermute(value, DPX, perm)

    passed = exchange(outer((3,), BF16), 1)
    given = exchange(outer((1,), BF16), 1)
    mine = outer((0, 2), F32)
    last = exchange((mine[1:] + passed.astype(F32)).astype(BF16), 2)
    total = mine[:1] + given.astype(F32) + last.astype(F32)
    return total.astype(BF16)[0]


def solution(mesh):
    return jax.shard_map(
        on_device,
        mesh=mesh,
        in_specs=(
            P("dp", "expert"),
            P("dp", "expert"),
            P("dp", None),
            P("dp", None),
            P("expert", None),
            P("expert", None),
            P("expert", None),
            P("expert", None),
        ),
        out_specs=P("expert", "dp"),
        check_vma=False,
    )
```
